32 devices in a mesh: cascade: 2 (over y), coil: 4 (over z), readout: 4 (over x, core).
Axes of the slice: x: 2, y: 2, z: 4, core: 2. Of those that a mesh axis runs over, the one named last changes fastest.
Arguments:
- initial: bfloat16 [2, 4, 8, 128, 2, 128], P(None, None, 'readout'), may hold values from -6 to 6
- coil_maps: bfloat16 [2, 16, 8, 128, 2, 128], P(None, 'coil', 'readout'), may hold values from -1.5 to 1.5
- kspace: bfloat16 [2, 16, 4, 8, 128, 2, 128], P(None, 'coil', None, 'readout'), may hold values from -6 to 6
- sampled: int32 [16, 4, 128, 128], P('coil'), may hold values 0 or 1
- first_w: bfloat16 [2, 27, 2, 64], P('cascade'), may hold values from -0.875 to 0.875
- time_w: bfloat16 [2, 3, 64, 64], P('cascade'), may hold values from -0.4375 to 0.4375
- last_w: bfloat16 [2, 27, 64, 2], P('cascade'), may hold values from -0.15625 to 0.15625
Outputs:
- images: bfloat16 [2, 2, 4, 8, 128, 2, 128], P('cascade', None, None, 'readout', 'coil')
The draws below stay inside these ranges and needn't reach their ends.
Inputs may be any that keep to these rules, and one draw needn't show every extreme that they name: `sampled`: 1 where the sample at that phase, line and partition was acquired for that coil, else 0.
All inputs are finite; a program needn't handle non-finite values. No bound on the sum of `sampled` on one device may be relied on, other than what follows from the above.
Results may differ from the reference program's by a relative error of at most 0.024.
Values may be sent and summed in bfloat16 or wider, within the bound.
No kernel may reach another device: no remote copies, remote signals or barrier semaphores. Data moves between devices by JAX's collectives and lax.ppermute only.
A program may use at most 128 MiB of HBM per device.

```python
import jax
import jax.numpy as jnp
from jax import lax

LINES = 128
PARTITIONS = 128
CHANNELS = 64
COILS = 16
PHASES = 4
MICRO = 2
CASCADES = 2
READOUT = 8


def set_ends(values, rng, smallest, top_value):
    index_at = [jax.random.randint(jax.random.fold_in(rng, axis), (), 0, length) for axis, length in enumerate(values.shape)]
    widest = values.shape.index(max(values.shape))
    beside = index_at[:widest] + [(index_at[widest] + 1) % values.shape[widest]] + index_at[widest + 1:]
    return values.at[tuple(index_at)].set(smallest).at[tuple(beside)].set(top_value)


def block_scale(rng, dims, pieces, low, largest):
    def one(dim, blocks):
        steps = jax.random.uniform(jax.random.fold_in(jax.random.fold_in(rng, 6), dim), (blocks,), jnp.float32, low / len(pieces), largest / len(pieces))
        return jnp.repeat(jnp.exp(steps), dims[dim] // blocks).reshape((-1,) + (1,) * (len(dims) - dim - 1))

    gain = one(*pieces[0])
    for cut in pieces[1:]:
        gain = gain * one(*cut)
    return gain


def centred(stream_key, extent, width, bound, shards=(), kind=jnp.bfloat16):
    factor_of = block_scale(stream_key, extent, shards, -0.22, 0.18) if shards else 1.0
    entries = jax.random.normal(stream_key, extent, jnp.float32) * width * factor_of
    return jnp.minimum(jnp.maximum(entries, -bound), bound).astype(kind)


def setup_inputs(seed: int = 0) -> dict:
    arg_keys = jax.random.split(jax.random.key(seed), 8)
    return {
        "initial": centred(arg_keys[0], (MICRO, PHASES, READOUT, LINES, 2, PARTITIONS), 1.0, 6.0, ((2, 4),)),
        "coil_maps": centred(arg_keys[1], (MICRO, COILS, READOUT, LINES, 2, PARTITIONS), 0.25, 1.5, ((1, 4), (2, 4))),
        "kspace": centred(arg_keys[2], (MICRO, COILS, PHASES, READOUT, LINES, 2, PARTITIONS), 1.0, 6.0, ((1, 4), (3, 4))),
        "sampled": set_ends((jax.random.randint(arg_keys[3], (COILS, PHASES, LINES, PARTITIONS), 0, 3) < 1).astype(jnp.int32), jax.random.fold_in(arg_keys[3], 1), 0, 1),
        "first_w": centred(arg_keys[4], (CASCADES, 27, 2, CHANNELS), 54 ** -0.5, 0.875, ((0, 2),)),
        "time_w": centred(arg_keys[5], (CASCADES, 3, CHANNELS, CHANNELS), (3 * CHANNELS) ** -0.5, 0.4375, ((0, 2),)),
        "last_w": centred(arg_keys[6], (CASCADES, 27, CHANNELS, 2), (27 * CHANNELS) ** -0.5, 0.15625, ((0, 2),)),
    }


def fourier_table(length, direction):
    positions = jnp.arange(length, dtype=jnp.int32)
    products = positions[:, None] * positions[None, :] % length
    angles = products.astype(jnp.float32) * (2.0 * jnp.pi / length)
    factor = 1.0 / jnp.sqrt(jnp.float32(length))
    return (jnp.cos(angles) * factor, direction * jnp.sin(angles) * factor)

def row_matrix(length, direction):
    cosine_part, sine_part = fourier_table(length, direction)
    blocks = jnp.stack([jnp.stack([cosine_part, -sine_part], -1), jnp.stack([sine_part, cosine_part], -1)], 1)
    return blocks.reshape(2 * length, 2 * length).astype(jnp.bfloat16)

def column_matrix(length, direction):
    cosine_part, sine_part = fourier_table(length, direction)
    blocks = jnp.stack([jnp.stack([cosine_part, sine_part], 1), jnp.stack([-sine_part, cosine_part], 1)], 0)
    return blocks.reshape(2 * length, 2 * length).astype(jnp.bfloat16)

def multiply(coil_map, values, conjugate):
    coil_map = coil_map.astype(jnp.float32)
    values = values.astype(jnp.float32)
    map_real, map_imag = (coil_map[..., 0, :], coil_map[..., 1, :])
    value_real, value_imag = (values[..., 0, :], values[..., 1, :])
    if conjugate:
        return jnp.stack([map_real * value_real + map_imag * value_imag, map_real * value_imag - map_imag * value_real], -2)
    return jnp.stack([map_real * value_real - map_imag * value_imag, map_real * value_imag + map_imag * value_real], -2)

def along_columns(fields, matrix):
    layout = fields.shape
    flattened = fields.reshape(-1, 2 * layout[-1])
    return jnp.dot(flattened, matrix, preferred_element_type=jnp.float32).reshape(layout)

def along_rows(fields, matrix):
    layout = fields.shape
    flattened = fields.reshape(-1, 2 * layout[-3], layout[-1]).astype(jnp.float32)
    result = jnp.einsum('ab,nbz->naz', matrix.astype(jnp.float32), flattened)
    return result.reshape(layout)

def coil_term(image, coil_map, coil_data, coil_mask, tables):
    forward_rows, forward_columns, inverse_rows, inverse_columns = tables
    coil_image = multiply(coil_map[None], image, False).astype(jnp.bfloat16)
    half_done = along_columns(coil_image, forward_columns).astype(jnp.bfloat16)
    spectrum = along_rows(half_done, forward_rows)
    weight = coil_mask.astype(jnp.float32)[:, None, :, None, :]
    mixed = (spectrum + weight * (coil_data.astype(jnp.float32) - spectrum)).astype(jnp.bfloat16)
    back_half = along_rows(mixed, inverse_rows).astype(jnp.bfloat16)
    restored = along_columns(back_half, inverse_columns)
    return multiply(coil_map[None], restored, True)

def lift(padded, weights):
    row_count = padded.shape[1] - 2
    line_count = padded.shape[2] - 2
    part_count = padded.shape[4] - 2
    tap_views = [padded[:, row_shift:row_shift + row_count, line_shift:line_shift + line_count, :, part_shift:part_shift + part_count] for row_shift in range(3) for line_shift in range(3) for part_shift in range(3)]
    stacked = jnp.stack(tap_views, 3)
    stacked = stacked.reshape(stacked.shape[0], row_count, line_count, -1, part_count)
    return jnp.einsum('prlie,io->prloe', stacked.astype(jnp.float32), weights.reshape(-1, weights.shape[-1]).astype(jnp.float32))

def temporal(hidden, weights):
    phase_count = hidden.shape[0]
    padded = jnp.pad(hidden, ((2, 2), (0, 0), (0, 0), (0, 0), (0, 0)))
    total = hidden.astype(jnp.float32)
    for tap_index in range(3):
        window = padded[2 * tap_index:2 * tap_index + phase_count].astype(jnp.float32)
        total = total + jnp.einsum('prlie,io->prloe', window, weights[tap_index].astype(jnp.float32))
    return jax.nn.relu(total).astype(jnp.bfloat16)

def project(edged, weights, base):
    row_count = edged.shape[1] - 2
    line_count = edged.shape[2] - 2
    part_count = edged.shape[4]
    per_tap = jnp.einsum('prlie,tio->prltoe', edged.astype(jnp.float32), weights.astype(jnp.float32))
    per_tap = jnp.pad(per_tap, ((0, 0), (0, 0), (0, 0), (0, 0), (0, 0), (1, 1)))
    total = base.astype(jnp.float32)
    for row_shift in range(3):
        for line_shift in range(3):
            for part_shift in range(3):
                tap_index = 9 * row_shift + 3 * line_shift + part_shift
                total = total + per_tap[:, row_shift:row_shift + row_count, line_shift:line_shift + line_count, tap_index, :, part_shift:part_shift + part_count]
    return total.astype(jnp.bfloat16)

def project_all(edged, weights, base):

    def one_phase(phase_pair):
        return project(phase_pair[0][None], weights, phase_pair[1][None])[0]
    return lax.map(one_phase, (edged, base))

def cascade(image, coil_maps, measured, sampled, first_w, time_w, last_w, tables):

    def add_coil(total, inputs):
        coil_map, coil_data, coil_mask = inputs
        return (total + coil_term(image, coil_map, coil_data, coil_mask, tables), None)
    combined, unused = lax.scan(add_coil, jnp.zeros(image.shape, jnp.float32), (coil_maps, measured, sampled))
    combined = combined.astype(jnp.bfloat16)
    padded = jnp.pad(combined, ((0, 0), (1, 1), (1, 1), (0, 0), (1, 1)))
    hidden = jax.nn.relu(lift(padded, first_w)).astype(jnp.bfloat16)
    mixed_time = temporal(hidden, time_w)
    edged = jnp.pad(mixed_time, ((0, 0), (1, 1), (1, 1), (0, 0), (0, 0)))
    return project_all(edged, last_w, combined)

def reference(initial, coil_maps, kspace, sampled, first_w, time_w, last_w):
    tables = (row_matrix(LINES, -1.0), column_matrix(PARTITIONS, -1.0), row_matrix(LINES, 1.0), column_matrix(PARTITIONS, 1.0))
    outputs_all = []
    for micro_index in range(MICRO):
        image = initial[micro_index]
        outputs_row = []
        for section_index in range(CASCADES):
            image = cascade(image, coil_maps[micro_index], kspace[micro_index], sampled, first_w[section_index], time_w[section_index], last_w[section_index], tables)
            outputs_row.append(image)
        outputs_all.append(jnp.stack(outputs_row))
    return jnp.stack(outputs_all, 1)
```

```python
import functools

import jax
import jax.numpy as jnp
import numpy as np
from jax import lax
from jax.experimental import pallas as pl
from jax.experimental.pallas import tpu as pltpu
from jax.sharding import PartitionSpec as P

F32 = jnp.float32
BF16 = jnp.bfloat16
HALO = 2
VMEM_LIMIT = 48 * 1024 * 1024


def fourier_pair(length):
    positions = np.arange(length, dtype=np.int64)
    angles = (positions[:, None] * positions[None, :] % length) * (2.0 * np.pi / length)
    factor = 1.0 / np.sqrt(float(length))
    return np.cos(angles) * factor, np.sin(angles) * factor


def times_i(length):
    turn = np.zeros((2 * length, 2 * length))
    even = 2 * np.arange(length)
    turn[even, even + 1] = -1.0
    turn[even + 1, even] = 1.0
    return turn


def row_matrix(length, direction):
    cosine, sine = fourier_pair(length)
    sine = direction * sine
    return np.stack([np.stack([cosine, -sine], -1), np.stack([sine, cosine], -1)], 1).reshape(
        2 * length, 2 * length
    )


def bf16(values):
    return jnp.asarray(values.astype(jnp.bfloat16))


@functools.lru_cache(maxsize=None)
def consistency_tables(line_total, part_total, phases, share):
    cosine, sine = fourier_pair(part_total)
    turn = times_i(line_total)
    forward, inverse = row_matrix(line_total, -1.0), row_matrix(line_total, 1.0)
    duplicate = np.repeat(np.eye(line_total), 2, axis=0)
    even = np.zeros((line_total, 2 * line_total))
    even[np.arange(line_total), 2 * np.arange(line_total)] = 1.0
    odd = np.roll(even, 1, axis=1)
    return (
        np.concatenate([cosine, sine], 1),
        np.concatenate([forward, -forward @ turn], 1),
        np.concatenate([inverse, turn @ inverse], 0),
        np.block([[cosine, -sine], [sine, cosine]]),
        np.concatenate([duplicate @ even, duplicate @ odd], 0),
        turn,
        duplicate,
        phase_inside(phases, share),
    )


def phase_inside(phases, share):
    rows = np.arange(phases * share * 2).reshape(phases, share, 2).transpose(1, 0, 2).reshape(-1)
    return np.eye(phases * share * 2)[rows]


def dot(left, right):
    return jnp.dot(left, right, preferred_element_type=F32)


def consistency_kernel(info, *refs, pieces, shares, coils, phases, share_rows, edge):
    images, refs = refs[:pieces], refs[pieces:]
    maps, samples, mask, cs, af, gg, ww, dd, turn, dup, inside = refs[:11]
    outs = refs[11 : 11 + shares]
    image_now, image_turned, total, window = refs[11 + shares :]
    coil = pl.program_id(1)
    me = info[1]
    part = maps.shape[-1]
    rows = maps.shape[-2]
    lanes = [slice(p * part, (p + 1) * part) for p in range(phases)]

    @pl.when(coil == 0)
    def _():
        if pieces == 1:
            image = jnp.concatenate([images[0][0, p, 0] for p in range(phases)], 1)
        else:
            joined = total
            for k in range(pieces):
                start = pl.multiple_of(lax.rem(me + (pieces - k), pieces) * share_rows, share_rows)
                for p in range(phases):
                    joined[pl.ds(start, share_rows), lanes[p]] = images[k][p, 0].astype(F32)
            image = joined[...].astype(BF16)
        image_now[...] = image.astype(F32)
        image_turned[...] = dot(turn[...], image)
        total[...] = jnp.zeros_like(total)

    both = dot(dd[...], maps[0, 0, 0])
    map_real, map_imag = both[:rows], both[rows:]
    fields = [
        (map_real * image_now[:, lanes[p]] + map_imag * image_turned[:, lanes[p]]).astype(BF16)
        for p in range(phases)
    ]
    halves = dot(jnp.concatenate(fields, 0), cs[...]).astype(BF16)
    stacked = jnp.concatenate(
        [
            jnp.concatenate(
                [halves[p * rows : (p + 1) * rows, :part], halves[p * rows : (p + 1) * rows, part:]], 0
            )
            for p in range(phases)
        ],
        1,
    )
    spectrum = dot(af[...], stacked)
    acquired = dot(
        dup[...], jnp.concatenate([mask[0, p].astype(F32).astype(BF16) for p in range(phases)], 1)
    )
    measured = jnp.concatenate([samples[0, 0, p, 0] for p in range(phases)], 1).astype(F32)
    mixed = jnp.where(acquired > 0.5, measured, spectrum).astype(BF16)
    back = dot(gg[...], mixed).astype(BF16)
    paired = jnp.concatenate(
        [jnp.concatenate([back[:rows, lanes[p]], back[rows:, lanes[p]]], 1) for p in range(phases)], 0
    )
    restored = dot(paired, ww[...])
    for p in range(phases):
        field = restored[p * rows : (p + 1) * rows]
        total[:, lanes[p]] += map_real * field[:, :part] - map_imag * field[:, part:]

    @pl.when(coil == coils - 1)
    def _():
        summed = total[...].astype(BF16)
        blocks = jnp.concatenate(
            [
                jnp.concatenate(
                    [summed[k * share_rows : (k + 1) * share_rows, lanes[p]] for p in range(phases)], 0
                )
                for k in range(shares)
            ],
            1,
        )
        ordered = dot(inside[...], blocks).astype(BF16)
        width = phases * share_rows
        border = jnp.zeros((edge, part), BF16)
        window[0:edge] = border
        window[edge + shares * width : 2 * edge + shares * width] = border
        for k in range(shares):
            window[edge + k * width : edge + (k + 1) * width] = ordered[:, k * part : (k + 1) * part]
        for k in range(shares):
            start = pl.multiple_of(lax.rem(me + k, shares) * width, width)
            outs[k][0] = window[pl.ds(start, width + 2 * edge)]


def consistency(info, images, maps, samples, mask, shares):
    blocks, coils, phases, readouts, rows, part = samples.shape
    lines = rows // 2
    share_rows = rows // shares
    edge = HALO * phases * 2
    tables = tuple(bf16(t) for t in consistency_tables(lines, part, phases, lines // shares))
    pieces = len(images)
    if pieces == 1:
        image_specs = [
            pl.BlockSpec((1, phases, 1, rows, part), lambda r, j, info: (info[0], 0, r, 0, 0))
        ]
    else:
        image_specs = [
            pl.BlockSpec((phases, 1, share_rows, part), lambda r, j, info: (0, r, 0, 0))
        ] * pieces
    fixed = [pl.BlockSpec(t.shape, lambda r, j, info: (0, 0)) for t in tables]
    width = phases * share_rows + 2 * edge
    body = functools.partial(
        consistency_kernel,
        pieces=pieces,
        shares=shares,
        coils=coils,
        phases=phases,
        share_rows=share_rows,
        edge=edge,
    )
    return pl.pallas_call(
        body,
        grid_spec=pltpu.PrefetchScalarGridSpec(
            num_scalar_prefetch=1,
            grid=(readouts, coils),
            in_specs=image_specs
            + [
                pl.BlockSpec((1, 1, 1, rows, part), lambda r, j, info: (info[0], j, r, 0, 0)),
                pl.BlockSpec(
                    (1, 1, phases, 1, rows, part), lambda r, j, info: (info[0], j, 0, r, 0, 0)
                ),
                pl.BlockSpec((1, phases, lines, part), lambda r, j, info: (j, 0, 0, 0)),
            ]
            + fixed,
            out_specs=[pl.BlockSpec((1, width, part), lambda r, j, info: (r, 0, 0))] * shares,
            scratch_shapes=[
                pltpu.VMEM((rows, phases * part), F32),
                pltpu.VMEM((rows, phases * part), F32),
                pltpu.VMEM((rows, phases * part), F32),
                pltpu.VMEM((shares * phases * share_rows + 2 * edge, part), BF16),
            ],
        ),
        out_shape=[jax.ShapeDtypeStruct((readouts, width, part), BF16)] * shares,
        compiler_params=pltpu.CompilerParams(vmem_limit_bytes=VMEM_LIMIT),
        cost_estimate=pl.CostEstimate(
            flops=readouts * coils * phases * rows * part * rows * 20,
            bytes_accessed=8 * 1024 * 1024,
            transcendentals=0,
        ),
        name="consistency",
    )(info, *images, maps, samples, mask, *tables)


def tap_rows(phases, parts):
    rows = []
    for row_shift in range(3):
        for tap in range(9):
            for phase in range(phases):
                for piece in range(parts):
                    rows.append(((9 * row_shift + tap) * parts + piece, phase))
        rows += [(-1, -1)] * (-(9 * phases * parts) % 16)
    return rows


@functools.lru_cache(maxsize=None)
def weight_tables(phases, channels):
    rows = tap_rows(phases, 2)
    spread = np.zeros((len(rows), 64))
    own_phase = np.zeros((len(rows), phases * channels))
    for index, (source, phase) in enumerate(rows):
        if source >= 0:
            spread[index, source] = 1.0
            own_phase[index, phase * channels : (phase + 1) * channels] = 1.0
    tiled = np.tile(np.eye(channels), (1, phases))
    phase_of = np.repeat(np.arange(phases), channels)
    time_masks = np.stack(
        [phase_of[None, :] - phase_of[:, None] == 2 * (k - 1) for k in range(3)]
    ).astype(np.float64)
    return spread, own_phase, tiled, time_masks


def weights_kernel(info, *refs, pieces):
    packs = refs[:pieces]
    spread, spread_t, own_phase, own_phase_t, tiled, tiled_t, time_masks = refs[pieces : pieces + 7]
    first_out, time_out, last_out = refs[pieces + 7 :]
    channels = tiled.shape[0]
    pick = lax.rem(info[0] - pl.program_id(0) + pieces, pieces)
    pack = packs[0][...].astype(F32)
    for k in range(1, pieces):
        pack = jnp.where(pick == k, packs[k][...].astype(F32), pack)
    pack = pack.astype(BF16)

    def transposed(block):
        return lax.dot_general(
            tiled_t[...], block, (((1,), (1,)), ((), ())), preferred_element_type=F32
        ).astype(BF16)

    time = 0.0
    for k in range(3):
        block = transposed(pack[k * channels : (k + 1) * channels])
        time = time + dot(block, tiled[...]) * time_masks[k].astype(F32)
    time_out[0] = time.astype(BF16)
    first = transposed(pack[3 * channels : 3 * channels + 64])
    first_out[0] = (dot(first, spread_t[...]) * own_phase_t[...].astype(F32)).astype(BF16)
    last = dot(spread[...], pack[3 * channels + 64 :]).astype(BF16)
    last_out[0] = (dot(last, tiled[...]) * own_phase[...].astype(F32)).astype(BF16)


def weight_matrices(info, packs, phases):
    sections = len(packs)
    channels = packs[0].shape[1]
    spread, own_phase, tiled, time_masks = weight_tables(phases, channels)
    tables = [
        bf16(t) for t in (spread, spread.T, own_phase, own_phase.T, tiled, tiled.T, time_masks)
    ]
    wide = phases * channels
    taps = spread.shape[0]
    shapes = [(wide, taps), (wide, wide), (taps, wide)]
    return pl.pallas_call(
        functools.partial(weights_kernel, pieces=sections),
        grid_spec=pltpu.PrefetchScalarGridSpec(
            num_scalar_prefetch=1,
            grid=(sections,),
            in_specs=[pl.BlockSpec(p.shape, lambda s, info: (0, 0)) for p in packs]
            + [
                pl.BlockSpec(t.shape, functools.partial(lambda n, s, info: (0,) * n, t.ndim))
                for t in tables
            ],
            out_specs=[pl.BlockSpec((1,) + s, lambda s, info: (s, 0, 0)) for s in shapes],
        ),
        out_shape=[jax.ShapeDtypeStruct((sections,) + s, BF16) for s in shapes],
        compiler_params=pltpu.CompilerParams(vmem_limit_bytes=VMEM_LIMIT),
        cost_estimate=pl.CostEstimate(
            flops=sections * wide * wide * 1000, bytes_accessed=2 * 1024 * 1024, transcendentals=0
        ),
        name="weights",
    )(info, *packs, *tables)


def shifted(values, step):
    part = values.shape[1]
    lane = lax.broadcasted_iota(jnp.int32, values.shape, 1)
    if step > 0:
        return jnp.where(lane == 0, 0.0, pltpu.roll(values, 1, 1))
    return jnp.where(lane == part - 1, 0.0, pltpu.roll(values, part - 1, 1))


def denoise_kernel(info, own, low, high, first, time, last, apart, out, taps, sums, *, phases, chunk):
    step = pl.program_id(0)
    steps = pl.num_programs(0)
    readouts, span, part = own.shape
    cell = 2 * phases
    lines = span // cell
    group = taps.shape[2]
    used = 9 * cell

    @pl.when(step == 0)
    def _():
        slabs = (
            [low[readouts - HALO + k] for k in range(HALO)]
            + [own[k] for k in range(readouts)]
            + [high[k] for k in range(HALO)]
        )
        filler = [jnp.zeros((group - used, part), F32)] if group > used else []
        for index, slab in enumerate(slabs):
            slab = slab.astype(F32)
            views = [shifted(slab, 1), slab, shifted(slab, -1)]
            for line in range(1, lines - 1):
                around = [
                    views[e][cell * (line + c - 1) : cell * (line + c)]
                    for c in range(3)
                    for e in range(3)
                ]
                taps[index, line - 1] = jnp.concatenate(around + filler, 0).astype(BF16)
        sums[...] = jnp.zeros_like(sums)

    inside = jnp.where(step == 0, info[2], jnp.where(step == steps - 1, info[3], 1))

    @pl.when(inside == 1)
    def _():
        for begin in range(1, lines - 1, chunk):
            block = range(begin, min(begin + chunk, lines - 1))
            near = jnp.concatenate(
                [taps[pl.ds(step, 3), line - 1].reshape(3 * group, part) for line in block], 1
            )
            hidden = jnp.maximum(dot(first[0], near), 0.0).astype(BF16)
            mixed = jnp.maximum(hidden.astype(F32) + dot(time[0], hidden), 0.0).astype(BF16)
            pieces = [mixed[:, k * part : (k + 1) * part] for k in range(len(block))]
            if block[0] == 1:
                pieces[0] = pieces[0] * info[4].astype(F32).astype(BF16)
            if block[-1] == lines - 2:
                pieces[-1] = pieces[-1] * info[5].astype(F32).astype(BF16)
            mixed = jnp.concatenate(pieces, 1)
            result = dot(last[0], mixed)
            for a in range(3):
                target = step + 2 - a
                for e in range(3):
                    for line in range(block[0] - 1, block[-1] + 2):
                        terms = []
                        for c in range(3):
                            source = line + c - 1
                            if block[0] <= source <= block[-1]:
                                at = a * group + (3 * c + e) * cell
                                k = source - block[0]
                                terms.append(result[at : at + cell, k * part : (k + 1) * part])
                        sums[e, target, line * cell : (line + 1) * cell] += sum(terms[1:], terms[0])

    @pl.when(step == steps - 1)
    def _():
        body = slice(HALO * cell, span - HALO * cell)
        finals = []
        for r in range(readouts):
            value = own[r, body].astype(F32) + sums[1, r + HALO, body]
            value = value + shifted(sums[0, r + HALO, body], 1)
            value = value + shifted(sums[2, r + HALO, body], -1)
            finals.append(value.astype(BF16))
        ordered = dot(apart[...], jnp.concatenate(finals, 1)).astype(BF16)
        height = out.shape[2]
        for p in range(phases):
            for r in range(readouts):
                out[p, r] = ordered[p * height : (p + 1) * height, r * part : (r + 1) * part]


def denoise(info, own, low, high, matrices, section, phases):
    readouts, span, part = own.shape
    cell = 2 * phases
    lines = span // cell
    share = lines - 2 * HALO
    first, time, last = matrices
    apart = bf16(phase_inside(phases, share).T)
    group = first.shape[2] // 3
    whole = pl.BlockSpec((readouts, span, part), lambda s, info: (0, 0, 0))
    return pl.pallas_call(
        functools.partial(denoise_kernel, phases=phases, chunk=17),
        grid_spec=pltpu.PrefetchScalarGridSpec(
            num_scalar_prefetch=1,
            grid=(readouts + 2,),
            in_specs=[whole] * 3
            + [pl.BlockSpec((1,) + w.shape[1:], lambda s, info: (section, 0, 0)) for w in matrices]
            + [pl.BlockSpec(apart.shape, lambda s, info: (0, 0))],
            out_specs=pl.BlockSpec((phases, readouts, 2 * share, part), lambda s, info: (0, 0, 0, 0)),
            scratch_shapes=[
                pltpu.VMEM((readouts + 2 * HALO, lines - 2, group, part), BF16),
                pltpu.VMEM((3, readouts + 2 * HALO, span, part), F32),
            ],
        ),
        out_shape=jax.ShapeDtypeStruct((phases, readouts, 2 * share, part), BF16),
        compiler_params=pltpu.CompilerParams(vmem_limit_bytes=VMEM_LIMIT),
        cost_estimate=pl.CostEstimate(
            flops=6 * (readouts + 2) * lines * part * 256 * 256,
            bytes_accessed=2 * 1024 * 1024,
            transcendentals=0,
        ),
        name="denoise",
    )(info, own, low, high, first, time, last, apart)


def rotation(count, step):
    return [(i, (i + step) % count) for i in range(count)]


def per_device(initial, coil_maps, kspace, sampled, first_w, time_w, last_w):
    section_no = lax.axis_index("cascade")
    sections = lax.axis_size("cascade")
    coil_no = lax.axis_index("coil")
    shares = lax.axis_size("coil")
    readout_no = lax.axis_index("readout")
    readout_parts = lax.axis_size("readout")
    phases = kspace.shape[2]
    part = kspace.shape[-1]
    channels = first_w.shape[-1]

    def rows_of(array):
        return array.reshape(array.shape[:-3] + (2 * array.shape[-3], part))

    initial, coil_maps, kspace = rows_of(initial), rows_of(coil_maps), rows_of(kspace)
    info = jnp.stack(
        [
            section_no,
            coil_no,
            readout_no > 0,
            readout_no < readout_parts - 1,
            coil_no > 0,
            coil_no < shares - 1,
        ]
    ).astype(jnp.int32)

    def padded(block):
        return jnp.pad(block, ((0, -block.shape[0] % 64), (0, 0)))

    pack = jnp.concatenate(
        [
            time_w[0].reshape(-1, channels),
            padded(first_w[0].reshape(-1, channels)),
            padded(jnp.swapaxes(last_w[0], 1, 2).reshape(-1, channels)),
        ],
        0,
    )
    packs = [pack] + [
        lax.ppermute(pack, "cascade", rotation(sections, k)) for k in range(1, sections)
    ]
    matrices = None
    images = [initial]
    outputs = []
    for section in range(sections):
        shares_out = consistency(info, images, coil_maps, kspace, sampled, shares)
        if matrices is None:
            packs, shares_out = lax.optimization_barrier((packs, shares_out))
        parts = [shares_out[0]] + [
            lax.ppermute(shares_out[k], "coil", rotation(shares, k)) for k in range(1, shares)
        ]
        if matrices is None:
            matrices = weight_matrices(info, packs, phases)
        combined = sum(p.astype(F32) for p in parts).astype(BF16)
        forward = [(i, i + 1) for i in range(readout_parts - 1)]
        backward = [(target, source) for source, target in forward]
        low = lax.ppermute(combined, "readout", forward)
        high = lax.ppermute(combined, "readout", backward)
        output = denoise(info, combined, low, high, matrices, section, phases)
        outputs.append(output)
        if section < sections - 1:
            images = [output] + [
                lax.ppermute(output, "coil", rotation(shares, k)) for k in range(1, shares)
            ]

    stacked = jnp.stack(outputs)
    placed = [lax.dynamic_index_in_dim(stacked, section_no, 0, False)]
    for k in range(1, sections):
        piece = lax.dynamic_index_in_dim(stacked, (section_no + k) % sections, 0, False)
        placed.append(lax.ppermute(piece, "cascade", rotation(sections, k)))
    arrived = []
    for block in range(sections):
        value = placed[0]
        for k in range(1, sections):
            value = jnp.where((section_no - block) % sections == k, placed[k], value)
        arrived.append(value)
    result = jnp.stack(arrived)[None]
    return result.reshape(result.shape[:-2] + (result.shape[-2] // 2, 2, part))


def solution(mesh):
    in_specs = (
        P(None, None, "readout", None, None, None),
        P(None, "coil", "readout", None, None, None),
        P(None, "coil", None, "readout", None, None, None),
        P("coil", None, None, None),
        P("cascade", None, None, None),
        P("cascade", None, None, None),
        P("cascade", None, None, None),
    )
    out_specs = P("cascade", None, None, "readout", "coil", None, None)
    return jax.shard_map(
        per_device, mesh=mesh, in_specs=in_specs, out_specs=out_specs, check_vma=False
    )
```

```python
import functools

import jax
import jax.numpy as jnp
import numpy as np
from jax import lax
from jax.experimental import pallas as pl
from jax.experimental.pallas import tpu as pltpu
from jax.sharding import PartitionSpec as P

F32 = jnp.float32
BF16 = jnp.bfloat16
HALO = 2
BATCH = 16
WIDE_LIMIT = 62 * 1024 * 1024
VMEM_LIMIT = 30 * 1024 * 1024


def fourier_pair(length):
    positions = np.arange(length, dtype=np.int64)
    angles = (positions[:, None] * positions[None, :] % length) * (2.0 * np.pi / length)
    factor = 1.0 / np.sqrt(float(length))
    return np.cos(angles) * factor, np.sin(angles) * factor


def bf16(values):
    return jnp.asarray(values.astype(jnp.bfloat16))


def column_matrix(length, direction):
    cosine, sine = fourier_pair(length)
    return np.block([[cosine, direction * sine], [-direction * sine, cosine]])


def parts_apart(length):
    rows = np.arange(2 * length).reshape(length, 2).T.reshape(-1)
    return np.eye(2 * length)[rows]


@functools.lru_cache(maxsize=None)
def consistency_tables(line_total, part_total, phases, share):
    tables = [
        column_matrix(part_total, -1.0),
        column_matrix(line_total, -1.0).T,
        column_matrix(line_total, 1.0).T,
        column_matrix(part_total, 1.0),
        parts_apart(line_total),
        line_major(phases, share),
    ]
    size = max(max(t.shape) for t in tables)
    stacked = np.zeros((len(tables), size, size))
    for index, table in enumerate(tables):
        stacked[index, : table.shape[0], : table.shape[1]] = table
    return stacked


def line_major(phases, share):
    rows = np.arange(phases * 2 * share).reshape(phases * 2, share).T.reshape(-1)
    return np.eye(phases * 2 * share)[rows]


def phase_inside(phases, share):
    rows = np.arange(phases * share * 2).reshape(phases, share, 2).transpose(1, 0, 2).reshape(-1)
    return np.eye(phases * share * 2)[rows]


def dot(left, right):
    return jnp.dot(left, right, preferred_element_type=F32)


def consistency_kernel(info, *refs, pieces, shares, edge, batch, direct):
    images, refs = refs[:pieces], refs[pieces:]
    maps, samples, mask, tables = refs[:4]
    outs = refs[4 : 4 + shares]
    window, joined, refs = refs[4 + shares], refs[5 + shares], refs[6 + shares :]
    block, me = info[0], info[1]
    coils, phases, readouts, rows, part = samples.shape[1:]
    count = rows // 2
    share = count // shares

    if direct:
        waits = {}
        maps, samples = maps.at[block], samples.at[block]
    else:
        sems = refs[-1]
        sources = (tables, images[0].at[block], maps.at[block], mask, samples.at[block])
        names = ("tables", "image", "maps", "mask", "samples")
        waits = {}
        for k, (name, source) in enumerate(zip(names, sources)):
            waits[name] = pltpu.make_async_copy(source, refs[k], sems.at[k])
            waits[name].start()
        tables, image, maps, mask, samples = refs[:5]

    def wait(name):
        if name in waits:
            waits.pop(name).wait()

    wait("tables")
    wait("image")
    if pieces > 1:
        image = joined
        for k in range(pieces):
            to = pl.multiple_of(lax.rem(me + (pieces - k), pieces) * 2 * share, 2 * share)
            joined[:, :, pl.ds(to, 2 * share)] = images[k][...]

    def apart(values):
        return dot(tables[4, :rows, :rows], values)

    def lane(n):
        return slice(n * part, (n + 1) * part)

    def band(n):
        return slice(n * count, (n + 1) * count)

    places = [(r, p) for r in range(readouts) for p in range(phases)]
    image_now = apart(jnp.concatenate([image[p, r] for r, p in places], 1))
    wait("maps")
    maps_now = apart(
        jnp.concatenate([maps[coil, r] for r in range(readouts) for coil in range(coils)], 1)
    )

    def map_parts(r, coil):
        where = lane(r * coils + coil)
        return maps_now[:count, where], maps_now[count:, where]

    slabs = [(r, coil, p) for r in range(readouts) for coil in range(coils) for p in range(phases)]
    real_sum = {place: 0.0 for place in places}
    imag_sum = {place: 0.0 for place in places}
    for begin in range(0, len(slabs), batch):
        group = slabs[begin : begin + batch]
        every = range(len(group))
        fields = []
        for r, coil, p in group:
            map_real, map_imag = map_parts(r, coil)
            where = lane(places.index((r, p)))
            real, imag = image_now[:count, where], image_now[count:, where]
            fields.append(
                jnp.concatenate(
                    [
                        (map_real * real - map_imag * imag).astype(BF16),
                        (map_real * imag + map_imag * real).astype(BF16),
                    ],
                    1,
                )
            )
        half = dot(jnp.concatenate(fields, 0), tables[0, : 2 * part, : 2 * part]).astype(BF16)
        stacked = jnp.concatenate(
            [jnp.concatenate([half[band(n), :part], half[band(n), part:]], 0) for n in every], 1
        )
        spectrum = dot(tables[1, :rows, :rows], stacked)
        wait("mask")
        wait("samples")
        measured = apart(jnp.concatenate([samples[coil, p, r] for r, coil, p in group], 1))
        acquired = jnp.concatenate([mask[coil, p] for r, coil, p in group], 1) != 0
        mixed = jnp.concatenate(
            [
                jnp.where(acquired, measured[:count], spectrum[:count]).astype(BF16),
                jnp.where(acquired, measured[count:], spectrum[count:]).astype(BF16),
            ],
            0,
        )
        back = dot(tables[2, :rows, :rows], mixed).astype(BF16)
        paired = jnp.concatenate(
            [jnp.concatenate([back[:count, lane(n)], back[count:, lane(n)]], 1) for n in every], 0
        )
        restored = dot(paired, tables[3, : 2 * part, : 2 * part])
        for n, (r, coil, p) in enumerate(group):
            map_real, map_imag = map_parts(r, coil)
            real, imag = restored[band(n), :part], restored[band(n), part:]
            real_sum[r, p] = real_sum[r, p] + (map_real * real + map_imag * imag)
            imag_sum[r, p] = imag_sum[r, p] + (map_real * imag - map_imag * real)

    blocks = []
    for r in range(readouts):
        summed = [
            v.astype(BF16) for p in range(phases) for v in (real_sum[r, p], imag_sum[r, p])
        ]
        blocks += [
            jnp.concatenate([v[k * share : (k + 1) * share] for v in summed], 0)
            for k in range(shares)
        ]
    width = phases * 2 * share
    ordered = dot(tables[5, :width, :width], jnp.concatenate(blocks, 1)).astype(BF16)
    border = jnp.zeros((edge, part), BF16)
    for r in range(readouts):
        window[r, 0:edge] = border
        window[r, edge + shares * width : 2 * edge + shares * width] = border
        for k in range(shares):
            window[r, edge + k * width : edge + (k + 1) * width] = ordered[:, lane(r * shares + k)]
    for k in range(shares):
        begin = pl.multiple_of(lax.rem(me + k, shares) * width, width)
        outs[k][...] = window[:, pl.ds(begin, width + 2 * edge)]


def consistency(info, images, maps, samples, mask, shares):
    blocks, coils, phases, readouts, rows, part = samples.shape
    lines = rows // 2
    share_rows = rows // shares
    edge = HALO * phases * 2
    tables = bf16(consistency_tables(lines, part, phases, lines // shares))
    pieces = len(images)
    direct = pieces > 1
    width = phases * share_rows + 2 * edge
    body = functools.partial(
        consistency_kernel, pieces=pieces, shares=shares, edge=edge, batch=BATCH, direct=direct
    )
    image_shape = (phases, readouts, rows, part)
    buffers = [
        pltpu.VMEM(tables.shape, BF16),
        pltpu.VMEM(image_shape, BF16),
        pltpu.VMEM((coils, readouts, rows, part), BF16),
        pltpu.VMEM((coils, phases, lines, part), jnp.int32),
        pltpu.VMEM((coils, phases, readouts, rows, part), BF16),
        pltpu.SemaphoreType.DMA((5,)),
    ]
    return pl.pallas_call(
        body,
        in_specs=[pl.BlockSpec(memory_space=pltpu.SMEM)]
        + [pl.BlockSpec(memory_space=pltpu.VMEM if direct else pl.ANY)] * (pieces + 4),
        out_specs=[pl.BlockSpec(memory_space=pltpu.VMEM)] * shares,
        scratch_shapes=[
            pltpu.VMEM((readouts, shares * phases * share_rows + 2 * edge, part), BF16),
            pltpu.VMEM(image_shape if direct else (16, part), BF16),
        ]
        + ([] if direct else buffers),
        out_shape=[jax.ShapeDtypeStruct((readouts, width, part), BF16)] * shares,
        compiler_params=pltpu.CompilerParams(
            vmem_limit_bytes=VMEM_LIMIT if direct else WIDE_LIMIT
        ),
        cost_estimate=pl.CostEstimate(
            flops=readouts * coils * phases * rows * part * rows * 20,
            bytes_accessed=4 * 1024 * 1024,
            transcendentals=0,
        ),
        name="consistency",
    )(info, *images, maps, samples, mask, tables)


def tap_rows(phases, parts):
    rows = []
    for row_shift in range(3):
        for tap in range(9):
            for phase in range(phases):
                for piece in range(parts):
                    rows.append(((9 * row_shift + tap) * parts + piece, phase))
        rows += [(-1, -1)] * (-(9 * phases * parts) % 16)
    return rows


@functools.lru_cache(maxsize=None)
def weight_tables(phases, channels):
    rows = tap_rows(phases, 2)
    spread = np.zeros((len(rows), 64))
    own_phase = np.zeros((len(rows), phases * channels))
    for index, (source, phase) in enumerate(rows):
        if source >= 0:
            spread[index, source] = 1.0
            own_phase[index, phase * channels : (phase + 1) * channels] = 1.0
    tiled = np.tile(np.eye(channels), (1, phases))
    phase_of = np.repeat(np.arange(phases), channels)
    time_masks = np.stack(
        [phase_of[None, :] - phase_of[:, None] == 2 * (k - 1) for k in range(3)]
    ).astype(np.float64)
    return spread, own_phase, tiled, time_masks


def weights_kernel(info, *refs, pieces):
    packs = refs[:pieces]
    spread, spread_t, own_phase, own_phase_t, tiled, tiled_t, time_masks = refs[pieces : pieces + 7]
    first_out, time_out, last_out = refs[pieces + 7 :]
    channels = tiled.shape[0]
    pick = lax.rem(info[0] - pl.program_id(0) + pieces, pieces)
    pack = packs[0][...].astype(F32)
    for k in range(1, pieces):
        pack = jnp.where(pick == k, packs[k][...].astype(F32), pack)
    pack = pack.astype(BF16)

    def transposed(block):
        return lax.dot_general(
            tiled_t[...], block, (((1,), (1,)), ((), ())), preferred_element_type=F32
        ).astype(BF16)

    time = 0.0
    for k in range(3):
        block = transposed(pack[k * channels : (k + 1) * channels])
        time = time + dot(block, tiled[...]) * time_masks[k].astype(F32)
    time_out[0] = time.astype(BF16)
    first = transposed(pack[3 * channels : 3 * channels + 64])
    first_out[0] = (dot(first, spread_t[...]) * own_phase_t[...].astype(F32)).astype(BF16)
    last = dot(spread[...], pack[3 * channels + 64 :]).astype(BF16)
    last_out[0] = (dot(last, tiled[...]) * own_phase[...].astype(F32)).astype(BF16)


def weight_matrices(info, packs, phases):
    sections = len(packs)
    channels = packs[0].shape[1]
    spread, own_phase, tiled, time_masks = weight_tables(phases, channels)
    tables = [
        bf16(t) for t in (spread, spread.T, own_phase, own_phase.T, tiled, tiled.T, time_masks)
    ]
    wide = phases * channels
    taps = spread.shape[0]
    shapes = [(wide, taps), (wide, wide), (taps, wide)]
    return pl.pallas_call(
        functools.partial(weights_kernel, pieces=sections),
        grid_spec=pltpu.PrefetchScalarGridSpec(
            num_scalar_prefetch=1,
            grid=(sections,),
            in_specs=[pl.BlockSpec(p.shape, lambda s, info: (0, 0)) for p in packs]
            + [
                pl.BlockSpec(t.shape, functools.partial(lambda n, s, info: (0,) * n, t.ndim))
                for t in tables
            ],
            out_specs=[pl.BlockSpec((1,) + s, lambda s, info: (s, 0, 0)) for s in shapes],
        ),
        out_shape=[jax.ShapeDtypeStruct((sections,) + s, BF16) for s in shapes],
        compiler_params=pltpu.CompilerParams(vmem_limit_bytes=VMEM_LIMIT),
        cost_estimate=pl.CostEstimate(
            flops=sections * wide * wide * 1000, bytes_accessed=2 * 1024 * 1024, transcendentals=0
        ),
        name="weights",
    )(info, *packs, *tables)


def shifted(values, step):
    part = values.shape[1]
    lane = lax.broadcasted_iota(jnp.int32, values.shape, 1)
    if step > 0:
        return jnp.where(lane == 0, 0.0, pltpu.roll(values, 1, 1))
    return jnp.where(lane == part - 1, 0.0, pltpu.roll(values, part - 1, 1))


def denoise_kernel(info, own, low, high, first, time, last, apart, out, taps, sums, *, phases, chunk):
    step = pl.program_id(0)
    steps = pl.num_programs(0)
    readouts, span, part = own.shape
    cell = 2 * phases
    lines = span // cell
    group = taps.shape[2]
    used = 9 * cell

    @pl.when(step == 0)
    def _():
        slabs = (
            [low[readouts - HALO + k] for k in range(HALO)]
            + [own[k] for k in range(readouts)]
            + [high[k] for k in range(HALO)]
        )
        filler = [jnp.zeros((group - used, part), F32)] if group > used else []
        for index, slab in enumerate(slabs):
            slab = slab.astype(F32)
            views = [shifted(slab, 1), slab, shifted(slab, -1)]
            for line in range(1, lines - 1):
                around = [
                    views[e][cell * (line + c - 1) : cell * (line + c)]
                    for c in range(3)
                    for e in range(3)
                ]
                taps[index, line - 1] = jnp.concatenate(around + filler, 0).astype(BF16)
        sums[...] = jnp.zeros_like(sums)

    used_taps = min(3, readouts)
    begun = jnp.clip(step - readouts + 1, 0, 3 - used_taps)
    inside = jnp.where(step == 0, info[2], jnp.where(step == steps - 1, info[3], 1))

    @pl.when(inside == 1)
    def _():
        for begin in range(1, lines - 1, chunk):
            block = range(begin, min(begin + chunk, lines - 1))
            near = jnp.concatenate(
                [taps[pl.ds(step, 3), line - 1].reshape(3 * group, part) for line in block], 1
            )
            hidden = jnp.maximum(dot(first[0], near), 0.0).astype(BF16)
            mixed = jnp.maximum(hidden.astype(F32) + dot(time[0], hidden), 0.0).astype(BF16)
            pieces = [mixed[:, k * part : (k + 1) * part] for k in range(len(block))]
            if block[0] == 1:
                pieces[0] = pieces[0] * info[4].astype(F32).astype(BF16)
            if block[-1] == lines - 2:
                pieces[-1] = pieces[-1] * info[5].astype(F32).astype(BF16)
            mixed = jnp.concatenate(pieces, 1)
            result = dot(last[0, pl.ds(pl.multiple_of(begun * group, 16), used_taps * group)], mixed)
            for a in range(used_taps):
                target = step + 2 - begun - a
                for e in range(3):
                    for line in range(block[0] - 1, block[-1] + 2):
                        terms = []
                        for c in range(3):
                            source = line + c - 1
                            if block[0] <= source <= block[-1]:
                                at = a * group + (3 * c + e) * cell
                                k = source - block[0]
                                terms.append(result[at : at + cell, k * part : (k + 1) * part])
                        sums[e, target, line * cell : (line + 1) * cell] += sum(terms[1:], terms[0])

    @pl.when(step == steps - 1)
    def _():
        body = slice(HALO * cell, span - HALO * cell)
        finals = []
        for r in range(readouts):
            value = own[r, body].astype(F32) + sums[1, r + HALO, body]
            value = value + shifted(sums[0, r + HALO, body], 1)
            value = value + shifted(sums[2, r + HALO, body], -1)
            finals.append(value.astype(BF16))
        ordered = dot(apart[...], jnp.concatenate(finals, 1)).astype(BF16)
        height = out.shape[2]
        for p in range(phases):
            for r in range(readouts):
                out[p, r] = ordered[p * height : (p + 1) * height, r * part : (r + 1) * part]


def denoise(info, own, low, high, matrices, section, phases):
    readouts, span, part = own.shape
    cell = 2 * phases
    lines = span // cell
    share = lines - 2 * HALO
    first, time, last = matrices
    apart = bf16(phase_inside(phases, share).T)
    group = first.shape[2] // 3
    whole = pl.BlockSpec((readouts, span, part), lambda s, info: (0, 0, 0))
    return pl.pallas_call(
        functools.partial(denoise_kernel, phases=phases, chunk=34),
        grid_spec=pltpu.PrefetchScalarGridSpec(
            num_scalar_prefetch=1,
            grid=(readouts + 2,),
            in_specs=[whole] * 3
            + [pl.BlockSpec((1,) + w.shape[1:], lambda s, info: (section, 0, 0)) for w in matrices]
            + [pl.BlockSpec(apart.shape, lambda s, info: (0, 0))],
            out_specs=pl.BlockSpec((phases, readouts, 2 * share, part), lambda s, info: (0, 0, 0, 0)),
            scratch_shapes=[
                pltpu.VMEM((readouts + 2 * HALO, lines - 2, group, part), BF16),
                pltpu.VMEM((3, readouts + 2 * HALO, span, part), F32),
            ],
        ),
        out_shape=jax.ShapeDtypeStruct((phases, readouts, 2 * share, part), BF16),
        compiler_params=pltpu.CompilerParams(vmem_limit_bytes=VMEM_LIMIT),
        cost_estimate=pl.CostEstimate(
            flops=6 * (readouts + 2) * lines * part * 256 * 256,
            bytes_accessed=2 * 1024 * 1024,
            transcendentals=0,
        ),
        name="denoise",
    )(info, own, low, high, first, time, last, apart)


def rotation(count, step):
    return [(i, (i + step) % count) for i in range(count)]


def per_device(initial, coil_maps, kspace, sampled, first_w, time_w, last_w):
    section_no = lax.axis_index("cascade")
    sections = lax.axis_size("cascade")
    coil_no = lax.axis_index("coil")
    shares = lax.axis_size("coil")
    readout_no = lax.axis_index("readout")
    readout_parts = lax.axis_size("readout")
    phases = kspace.shape[2]
    part = kspace.shape[-1]
    channels = first_w.shape[-1]

    def rows_of(array):
        return array.reshape(array.shape[:-3] + (2 * array.shape[-3], part))

    initial, coil_maps, kspace = rows_of(initial), rows_of(coil_maps), rows_of(kspace)
    info = jnp.stack(
        [
            section_no,
            coil_no,
            readout_no > 0,
            readout_no < readout_parts - 1,
            coil_no > 0,
            coil_no < shares - 1,
        ]
    ).astype(jnp.int32)

    def padded(block):
        return jnp.pad(block, ((0, -block.shape[0] % 64), (0, 0)))

    def exchanged(values, axis, count):
        return [values[0]] + [
            lax.ppermute(values[k], axis, rotation(count, k)) for k in range(1, count)
        ]

    forward = [(i, i + 1) for i in range(readout_parts - 1)]
    backward = [(target, source) for source, target in forward]
    images = [initial]
    matrices = None
    kept, sent = [], []
    for section in range(sections):
        partial = consistency(info, images, coil_maps, kspace, sampled, shares)
        if matrices is None:
            partial, (first_w, time_w, last_w) = lax.optimization_barrier(
                (partial, (first_w, time_w, last_w))
            )
        parts = exchanged(partial, "coil", shares)
        if matrices is None:
            pack = jnp.concatenate(
                [
                    time_w[0].reshape(-1, channels),
                    padded(first_w[0].reshape(-1, channels)),
                    padded(jnp.swapaxes(last_w[0], 1, 2).reshape(-1, channels)),
                ],
                0,
            )
            packs = exchanged([pack] * sections, "cascade", sections)
            matrices = weight_matrices(info, packs, phases)
        combined = sum(p.astype(F32) for p in parts).astype(BF16)
        low = lax.ppermute(combined, "readout", forward)
        high = lax.ppermute(combined, "readout", backward)
        output = denoise(info, combined, low, high, matrices, section, phases)
        if section < sections - 1:
            images = exchanged([output] * shares, "coil", shares)
        kept.append(output)
        sent.append(
            [
                lax.ppermute(output, "cascade", [((section + k) % sections, section)])
                for k in range(1, sections)
            ]
        )

    arrived = []
    for block in range(sections):
        value = None
        for section in range(sections):
            k = (block - section) % sections
            piece = sent[section][k - 1] if k else kept[section]
            value = piece if value is None else jnp.where(section_no == section, piece, value)
        arrived.append(value)
    result = jnp.stack(arrived)[None]
    return result.reshape(result.shape[:-2] + (result.shape[-2] // 2, 2, part))


def solution(mesh):
    in_specs = (
        P(None, None, "readout", None, None, None),
        P(None, "coil", "readout", None, None, None),
        P(None, "coil", None, "readout", None, None, None),
        P("coil", None, None, None),
        P("cascade", None, None, None),
        P("cascade", None, None, None),
        P("cascade", None, None, None),
    )
    out_specs = P("cascade", None, None, "readout", "coil", None, None)
    return jax.shard_map(
        per_device, mesh=mesh, in_specs=in_specs, out_specs=out_specs, check_vma=False
    )
```

```python
import functools

import jax
import jax.numpy as jnp
import numpy as np
from jax import lax
from jax.experimental import pallas as pl
from jax.experimental.pallas import tpu as pltpu
from jax.sharding import PartitionSpec as P

F32 = jnp.float32
BF16 = jnp.bfloat16
HALO = 2
BATCH = 16
WIDE_LIMIT = 62 * 1024 * 1024
VMEM_LIMIT = 30 * 1024 * 1024


def fourier_pair(length):
    positions = np.arange(length, dtype=np.int64)
    angles = (positions[:, None] * positions[None, :] % length) * (2.0 * np.pi / length)
    factor = 1.0 / np.sqrt(float(length))
    return np.cos(angles) * factor, np.sin(angles) * factor


def bf16(values):
    return jnp.asarray(values.astype(jnp.bfloat16))


def column_matrix(length, direction):
    cosine, sine = fourier_pair(length)
    return np.block([[cosine, direction * sine], [-direction * sine, cosine]])


def parts_apart(length):
    rows = np.arange(2 * length).reshape(length, 2).T.reshape(-1)
    return np.eye(2 * length)[rows]


@functools.lru_cache(maxsize=None)
def consistency_tables(line_total, part_total, phases, share):
    tables = [
        column_matrix(part_total, -1.0),
        column_matrix(line_total, -1.0).T,
        column_matrix(line_total, 1.0).T,
        column_matrix(part_total, 1.0),
        parts_apart(line_total),
        line_major(phases, share),
    ]
    size = max(max(t.shape) for t in tables)
    stacked = np.zeros((len(tables), size, size))
    for index, table in enumerate(tables):
        stacked[index, : table.shape[0], : table.shape[1]] = table
    return stacked


def line_major(phases, share):
    rows = np.arange(phases * 2 * share).reshape(phases * 2, share).T.reshape(-1)
    return np.eye(phases * 2 * share)[rows]


def phase_inside(phases, share):
    rows = np.arange(phases * share * 2).reshape(phases, share, 2).transpose(1, 0, 2).reshape(-1)
    return np.eye(phases * share * 2)[rows]


def dot(left, right):
    return jnp.dot(left, right, preferred_element_type=F32)


def consistency_kernel(*refs, pieces, shares, edge, batch, direct):
    images, refs = refs[:pieces], refs[pieces:]
    maps, samples, mask, tables = refs[:4]
    outs = refs[4 : 4 + shares]
    window, joined, refs = refs[4 + shares], refs[5 + shares], refs[6 + shares :]
    block, me = lax.axis_index("cascade"), lax.axis_index("coil")
    coils, phases, readouts, rows, part = samples.shape[1:]
    count = rows // 2
    share = count // shares

    if direct:
        waits = {}
        maps, samples = maps.at[block], samples.at[block]
    else:
        sems = refs[-1]
        sources = (tables, images[0].at[block], maps.at[block], mask, samples.at[block])
        names = ("tables", "image", "maps", "mask", "samples")
        waits = {}
        for k, (name, source) in enumerate(zip(names, sources)):
            waits[name] = pltpu.make_async_copy(source, refs[k], sems.at[k])
            waits[name].start()
        tables, image, maps, mask, samples = refs[:5]

    def wait(name):
        if name in waits:
            waits.pop(name).wait()

    wait("tables")
    wait("image")
    if pieces > 1:
        image = joined
        for k in range(pieces):
            to = pl.multiple_of(lax.rem(me + (pieces - k), pieces) * 2 * share, 2 * share)
            joined[:, :, pl.ds(to, 2 * share)] = images[k][...]

    def apart(values):
        return dot(tables[4, :rows, :rows], values)

    def lane(n):
        return slice(n * part, (n + 1) * part)

    def band(n):
        return slice(n * count, (n + 1) * count)

    places = [(r, p) for r in range(readouts) for p in range(phases)]
    image_now = apart(jnp.concatenate([image[p, r] for r, p in places], 1))
    wait("maps")
    maps_now = apart(
        jnp.concatenate([maps[coil, r] for r in range(readouts) for coil in range(coils)], 1)
    )

    def map_parts(r, coil):
        where = lane(r * coils + coil)
        return maps_now[:count, where], maps_now[count:, where]

    slabs = [(r, coil, p) for r in range(readouts) for coil in range(coils) for p in range(phases)]
    real_sum = {place: 0.0 for place in places}
    imag_sum = {place: 0.0 for place in places}
    for begin in range(0, len(slabs), batch):
        group = slabs[begin : begin + batch]
        every = range(len(group))
        fields = []
        for r, coil, p in group:
            map_real, map_imag = map_parts(r, coil)
            where = lane(places.index((r, p)))
            real, imag = image_now[:count, where], image_now[count:, where]
            fields.append(
                jnp.concatenate(
                    [
                        (map_real * real - map_imag * imag).astype(BF16),
                        (map_real * imag + map_imag * real).astype(BF16),
                    ],
                    1,
                )
            )
        half = dot(jnp.concatenate(fields, 0), tables[0, : 2 * part, : 2 * part]).astype(BF16)
        stacked = jnp.concatenate(
            [jnp.concatenate([half[band(n), :part], half[band(n), part:]], 0) for n in every], 1
        )
        spectrum = dot(tables[1, :rows, :rows], stacked)
        wait("mask")
        wait("samples")
        measured = apart(jnp.concatenate([samples[coil, p, r] for r, coil, p in group], 1))
        acquired = jnp.concatenate([mask[coil, p] for r, coil, p in group], 1) != 0
        mixed = jnp.concatenate(
            [
                jnp.where(acquired, measured[:count], spectrum[:count]).astype(BF16),
                jnp.where(acquired, measured[count:], spectrum[count:]).astype(BF16),
            ],
            0,
        )
        back = dot(tables[2, :rows, :rows], mixed).astype(BF16)
        paired = jnp.concatenate(
            [jnp.concatenate([back[:count, lane(n)], back[count:, lane(n)]], 1) for n in every], 0
        )
        restored = dot(paired, tables[3, : 2 * part, : 2 * part])
        for n, (r, coil, p) in enumerate(group):
            map_real, map_imag = map_parts(r, coil)
            real, imag = restored[band(n), :part], restored[band(n), part:]
            real_sum[r, p] = real_sum[r, p] + (map_real * real + map_imag * imag)
            imag_sum[r, p] = imag_sum[r, p] + (map_real * imag - map_imag * real)

    blocks = []
    for r in range(readouts):
        summed = [
            v.astype(BF16) for p in range(phases) for v in (real_sum[r, p], imag_sum[r, p])
        ]
        blocks += [
            jnp.concatenate([v[k * share : (k + 1) * share] for v in summed], 0)
            for k in range(shares)
        ]
    width = phases * 2 * share
    ordered = dot(tables[5, :width, :width], jnp.concatenate(blocks, 1)).astype(BF16)
    border = jnp.zeros((edge, part), BF16)
    for r in range(readouts):
        window[r, 0:edge] = border
        window[r, edge + shares * width : 2 * edge + shares * width] = border
        for k in range(shares):
            window[r, edge + k * width : edge + (k + 1) * width] = ordered[:, lane(r * shares + k)]
    for k in range(shares):
        begin = pl.multiple_of(lax.rem(me + k, shares) * width, width)
        outs[k][...] = window[:, pl.ds(begin, width + 2 * edge)]


def consistency(images, maps, samples, mask, shares):
    blocks, coils, phases, readouts, rows, part = samples.shape
    lines = rows // 2
    share_rows = rows // shares
    edge = HALO * phases * 2
    tables = bf16(consistency_tables(lines, part, phases, lines // shares))
    pieces = len(images)
    direct = pieces > 1
    width = phases * share_rows + 2 * edge
    body = functools.partial(
        consistency_kernel, pieces=pieces, shares=shares, edge=edge, batch=BATCH, direct=direct
    )
    image_shape = (phases, readouts, rows, part)
    buffers = [
        pltpu.VMEM(tables.shape, BF16),
        pltpu.VMEM(image_shape, BF16),
        pltpu.VMEM((coils, readouts, rows, part), BF16),
        pltpu.VMEM((coils, phases, lines, part), jnp.int32),
        pltpu.VMEM((coils, phases, readouts, rows, part), BF16),
        pltpu.SemaphoreType.DMA((5,)),
    ]
    return pl.pallas_call(
        body,
        in_specs=[pl.BlockSpec(memory_space=pltpu.VMEM if direct else pl.ANY)] * (pieces + 4),
        out_specs=[pl.BlockSpec(memory_space=pltpu.VMEM)] * shares,
        scratch_shapes=[
            pltpu.VMEM((readouts, shares * phases * share_rows + 2 * edge, part), BF16),
            pltpu.VMEM(image_shape if direct else (16, part), BF16),
        ]
        + ([] if direct else buffers),
        out_shape=[jax.ShapeDtypeStruct((readouts, width, part), BF16)] * shares,
        compiler_params=pltpu.CompilerParams(
            vmem_limit_bytes=VMEM_LIMIT if direct else WIDE_LIMIT
        ),
        cost_estimate=pl.CostEstimate(
            flops=readouts * coils * phases * rows * part * rows * 20,
            bytes_accessed=4 * 1024 * 1024,
            transcendentals=0,
        ),
        name="consistency",
    )(*images, maps, samples, mask, tables)


def tap_rows(phases, parts):
    rows = []
    for row_shift in range(3):
        for tap in range(9):
            for phase in range(phases):
                for piece in range(parts):
                    rows.append(((9 * row_shift + tap) * parts + piece, phase))
        rows += [(-1, -1)] * (-(9 * phases * parts) % 16)
    return rows


@functools.lru_cache(maxsize=None)
def weight_tables(phases, channels):
    rows = tap_rows(phases, 2)
    spread = np.zeros((len(rows), 64))
    own_phase = np.zeros((len(rows), phases * channels))
    for index, (source, phase) in enumerate(rows):
        if source >= 0:
            spread[index, source] = 1.0
            own_phase[index, phase * channels : (phase + 1) * channels] = 1.0
    tiled = np.tile(np.eye(channels), (1, phases))
    phase_of = np.repeat(np.arange(phases), channels)
    time_masks = np.stack(
        [phase_of[None, :] - phase_of[:, None] == 2 * (k - 1) for k in range(3)]
    ).astype(np.float64)
    return spread, own_phase, tiled, time_masks


def weights_kernel(*refs, pieces):
    packs = refs[:pieces]
    spread, spread_t, own_phase, own_phase_t, tiled, tiled_t, time_masks = refs[pieces : pieces + 7]
    first_out, time_out, last_out = refs[pieces + 7 :]
    channels = tiled.shape[0]
    me = lax.axis_index("cascade")

    def transposed(block):
        return lax.dot_general(
            tiled_t[...], block, (((1,), (1,)), ((), ())), preferred_element_type=F32
        ).astype(BF16)

    for section in range(pieces):
        pick = lax.rem(me - section + pieces, pieces)
        pack = packs[0][...].astype(F32)
        for k in range(1, pieces):
            pack = jnp.where(pick == k, packs[k][...].astype(F32), pack)
        pack = pack.astype(BF16)
        time = 0.0
        for k in range(3):
            block = transposed(pack[k * channels : (k + 1) * channels])
            time = time + dot(block, tiled[...]) * time_masks[k].astype(F32)
        time_out[section] = time.astype(BF16)
        first = transposed(pack[3 * channels : 3 * channels + 64])
        first_out[section] = (dot(first, spread_t[...]) * own_phase_t[...].astype(F32)).astype(BF16)
        last = dot(spread[...], pack[3 * channels + 64 :]).astype(BF16)
        last_out[section] = (dot(last, tiled[...]) * own_phase[...].astype(F32)).astype(BF16)


def weight_matrices(packs, phases):
    sections = len(packs)
    channels = packs[0].shape[1]
    spread, own_phase, tiled, time_masks = weight_tables(phases, channels)
    tables = [
        bf16(t) for t in (spread, spread.T, own_phase, own_phase.T, tiled, tiled.T, time_masks)
    ]
    wide = phases * channels
    taps = spread.shape[0]
    shapes = [(wide, taps), (wide, wide), (taps, wide)]
    return pl.pallas_call(
        functools.partial(weights_kernel, pieces=sections),
        in_specs=[pl.BlockSpec(memory_space=pltpu.VMEM)] * (sections + len(tables)),
        out_specs=[pl.BlockSpec(memory_space=pltpu.VMEM)] * len(shapes),
        out_shape=[jax.ShapeDtypeStruct((sections,) + s, BF16) for s in shapes],
        compiler_params=pltpu.CompilerParams(vmem_limit_bytes=VMEM_LIMIT),
        cost_estimate=pl.CostEstimate(
            flops=sections * wide * wide * 1000, bytes_accessed=2 * 1024 * 1024, transcendentals=0
        ),
        name="weights",
    )(*packs, *tables)


def shifted(values, step):
    part = values.shape[1]
    lane = lax.broadcasted_iota(jnp.int32, values.shape, 1)
    if step > 0:
        return jnp.where(lane == 0, 0.0, pltpu.roll(values, 1, 1))
    return jnp.where(lane == part - 1, 0.0, pltpu.roll(values, part - 1, 1))


def denoise_kernel(own, even, odd, first, time, last, apart, out, taps, sums, *, phases, section):
    readouts, span, part = own.shape
    cell = 2 * phases
    lines = span // cell
    group = taps.shape[2]
    used = 9 * cell
    steps = readouts + 2
    readout_no, coil_no = lax.axis_index("readout"), lax.axis_index("coil")
    low_inside = readout_no > 0
    high_inside = readout_no < lax.axis_size("readout") - 1
    first_line = (coil_no > 0).astype(F32).astype(BF16)
    last_line = (coil_no < lax.axis_size("coil") - 1).astype(F32).astype(BF16)
    swapped = lax.rem(readout_no, 2) == 1

    def side(inside, here, there):
        return jnp.where(inside, jnp.where(swapped, here.astype(F32), there.astype(F32)), 0.0)

    slabs = (
        [side(low_inside, even[readouts - HALO + k], odd[readouts - HALO + k]) for k in range(HALO)]
        + [own[k].astype(F32) for k in range(readouts)]
        + [side(high_inside, odd[k], even[k]) for k in range(HALO)]
    )
    filler = [jnp.zeros((group - used, part), F32)] if group > used else []
    for index, slab in enumerate(slabs):
        views = [shifted(slab, 1), slab, shifted(slab, -1)]
        for line in range(1, lines - 1):
            around = [
                views[e][cell * (line + c - 1) : cell * (line + c)] for c in range(3) for e in range(3)
            ]
            taps[index, line - 1] = jnp.concatenate(around + filler, 0).astype(BF16)
    sums[...] = jnp.zeros_like(sums)
    used_taps = min(3, readouts)

    def add_row(step, carry):
        begun = jnp.clip(step - readouts + 1, 0, 3 - used_taps)
        inside = ((step > 0) | low_inside) & ((step < steps - 1) | high_inside)

        @pl.when(inside)
        def _():
            block = range(1, lines - 1)
            near = jnp.concatenate(
                [taps[pl.ds(step, 3), line - 1].reshape(3 * group, part) for line in block], 1
            )
            hidden = jnp.maximum(dot(first[section], near), 0.0).astype(BF16)
            mixed = jnp.maximum(hidden.astype(F32) + dot(time[section], hidden), 0.0).astype(BF16)
            edge = (len(block) - 1) * part
            mixed = jnp.concatenate(
                [mixed[:, :part] * first_line, mixed[:, part:edge], mixed[:, edge:] * last_line], 1
            )
            chosen = pl.ds(pl.multiple_of(begun * group, 16), used_taps * group)
            result = dot(last[section, chosen], mixed)
            for a in range(used_taps):
                target = step + 2 - begun - a
                for e in range(3):
                    for line in range(lines):
                        terms = []
                        for c in range(3):
                            source = line + c - 2
                            if 0 <= source < len(block):
                                at = a * group + (3 * c + e) * cell
                                terms.append(
                                    result[at : at + cell, source * part : (source + 1) * part]
                                )
                        sums[e, target, line * cell : (line + 1) * cell] += sum(terms[1:], terms[0])

        return carry

    lax.fori_loop(0, steps, add_row, 0)

    body = slice(HALO * cell, span - HALO * cell)
    finals = []
    for r in range(readouts):
        value = own[r, body].astype(F32) + sums[1, r + HALO, body]
        value = value + shifted(sums[0, r + HALO, body], 1)
        value = value + shifted(sums[2, r + HALO, body], -1)
        finals.append(value.astype(BF16))
    ordered = dot(apart[...], jnp.concatenate(finals, 1)).astype(BF16)
    height = out.shape[2]
    for p in range(phases):
        for r in range(readouts):
            out[p, r] = ordered[p * height : (p + 1) * height, r * part : (r + 1) * part]


def denoise(own, even, odd, matrices, section, phases):
    readouts, span, part = own.shape
    cell = 2 * phases
    lines = span // cell
    share = lines - 2 * HALO
    apart = bf16(phase_inside(phases, share).T)
    group = matrices[0].shape[2] // 3
    return pl.pallas_call(
        functools.partial(denoise_kernel, phases=phases, section=section),
        in_specs=[pl.BlockSpec(memory_space=pltpu.VMEM)] * 7,
        out_specs=pl.BlockSpec(memory_space=pltpu.VMEM),
        scratch_shapes=[
            pltpu.VMEM((readouts + 2 * HALO, lines - 2, group, part), BF16),
            pltpu.VMEM((3, readouts + 2 * HALO, span, part), F32),
        ],
        out_shape=jax.ShapeDtypeStruct((phases, readouts, 2 * share, part), BF16),
        compiler_params=pltpu.CompilerParams(vmem_limit_bytes=VMEM_LIMIT),
        cost_estimate=pl.CostEstimate(
            flops=6 * (readouts + 2) * lines * part * 256 * 256,
            bytes_accessed=2 * 1024 * 1024,
            transcendentals=0,
        ),
        name="denoise",
    )(own, even, odd, *matrices, apart)


def rotation(count, step):
    return [(i, (i + step) % count) for i in range(count)]


def swaps(count, first):
    pairs = [(i, i + 1) for i in range(first, count - 1, 2)]
    return pairs + [(target, source) for source, target in pairs]


def exchanged(values, axis, count):
    arrived = {0: values[0]}
    for k in sorted(range(1, count), key=lambda k: abs(k - count / 2)):
        arrived[k] = lax.ppermute(values[k], axis, rotation(count, k))
    return [arrived[k] for k in range(count)]


def per_device(initial, coil_maps, kspace, sampled, first_w, time_w, last_w):
    section_no = lax.axis_index("cascade")
    sections = lax.axis_size("cascade")
    shares = lax.axis_size("coil")
    readout_parts = lax.axis_size("readout")
    phases = kspace.shape[2]
    part = kspace.shape[-1]
    channels = first_w.shape[-1]

    def rows_of(array):
        return array.reshape(array.shape[:-3] + (2 * array.shape[-3], part))

    def padded(block):
        return jnp.pad(block, ((0, -block.shape[0] % 64), (0, 0)))

    initial, coil_maps, kspace = rows_of(initial), rows_of(coil_maps), rows_of(kspace)
    images = [initial]
    matrices = None
    kept, sent = [], []
    for section in range(sections):
        partial = consistency(images, coil_maps, kspace, sampled, shares)
        if matrices is None:
            partial, (first_w, time_w, last_w) = lax.optimization_barrier(
                (partial, (first_w, time_w, last_w))
            )
        parts = exchanged(partial, "coil", shares)
        if matrices is None:
            pack = jnp.concatenate(
                [
                    time_w[0].reshape(-1, channels),
                    padded(first_w[0].reshape(-1, channels)),
                    padded(jnp.swapaxes(last_w[0], 1, 2).reshape(-1, channels)),
                ],
                0,
            )
            packs = exchanged([pack] * sections, "cascade", sections)
            matrices = weight_matrices(packs, phases)
            parts, matrices = lax.optimization_barrier((parts, matrices))
        else:
            parts, sent[-1] = lax.optimization_barrier((parts, sent[-1]))
        combined = sum(p.astype(F32) for p in parts).astype(BF16)
        even = lax.ppermute(combined, "readout", swaps(readout_parts, 0))
        odd = lax.ppermute(combined, "readout", swaps(readout_parts, 1))
        output = denoise(combined, even, odd, matrices, section, phases)
        if section < sections - 1:
            images = exchanged([output] * shares, "coil", shares)
        kept.append(output)
        sent.append(
            [
                lax.ppermute(output, "cascade", [((section + k) % sections, section)])
                for k in range(1, sections)
            ]
        )

    arrived = []
    for block in range(sections):
        value = None
        for section in range(sections):
            k = (block - section) % sections
            piece = sent[section][k - 1] if k else kept[section]
            value = piece if value is None else jnp.where(section_no == section, piece, value)
        arrived.append(value)
    result = jnp.stack(arrived)[None]
    return result.reshape(result.shape[:-2] + (result.shape[-2] // 2, 2, part))


def solution(mesh):
    in_specs = (
        P(None, None, "readout", None, None, None),
        P(None, "coil", "readout", None, None, None),
        P(None, "coil", None, "readout", None, None, None),
        P("coil", None, None, None),
        P("cascade", None, None, None),
        P("cascade", None, None, None),
        P("cascade", None, None, None),
    )
    out_specs = P("cascade", None, None, "readout", "coil", None, None)
    return jax.shard_map(
        per_device, mesh=mesh, in_specs=in_specs, out_specs=out_specs, check_vma=False
    )
```

```python
import functools

import jax
import jax.numpy as jnp
import numpy as np
from jax import lax
from jax.experimental import pallas as pl
from jax.experimental.pallas import tpu as pltpu
from jax.sharding import PartitionSpec as P

F32 = jnp.float32
BF16 = jnp.bfloat16
HALO = 2
BATCH = 16
WIDE_LIMIT = 62 * 1024 * 1024
VMEM_LIMIT = 30 * 1024 * 1024


def fourier_pair(length):
    positions = np.arange(length, dtype=np.int64)
    angles = (positions[:, None] * positions[None, :] % length) * (2.0 * np.pi / length)
    factor = 1.0 / np.sqrt(float(length))
    return np.cos(angles) * factor, np.sin(angles) * factor


def bf16(values):
    return jnp.asarray(values.astype(jnp.bfloat16))


def column_matrix(length, direction):
    cosine, sine = fourier_pair(length)
    return np.block([[cosine, direction * sine], [-direction * sine, cosine]])


def parts_apart(length):
    rows = np.arange(2 * length).reshape(length, 2).T.reshape(-1)
    return np.eye(2 * length)[rows]


@functools.lru_cache(maxsize=None)
def consistency_tables(line_total, part_total, phases, share):
    tables = [
        column_matrix(part_total, -1.0),
        column_matrix(line_total, -1.0).T,
        column_matrix(line_total, 1.0).T,
        column_matrix(part_total, 1.0),
        parts_apart(line_total),
        line_major(phases, share),
    ]
    size = max(max(t.shape) for t in tables)
    stacked = np.zeros((len(tables), size, size))
    for index, table in enumerate(tables):
        stacked[index, : table.shape[0], : table.shape[1]] = table
    return stacked


def line_major(phases, share):
    rows = np.arange(phases * 2 * share).reshape(phases * 2, share).T.reshape(-1)
    return np.eye(phases * 2 * share)[rows]


def phase_inside(phases, share):
    rows = np.arange(phases * share * 2).reshape(phases, share, 2).transpose(1, 0, 2).reshape(-1)
    return np.eye(phases * share * 2)[rows]


def dot(left, right):
    return jnp.dot(left, right, preferred_element_type=F32)


def consistency_kernel(*refs, pieces, shares, edge, batch, direct):
    images, refs = refs[:pieces], refs[pieces:]
    maps, samples, mask, tables = refs[:4]
    outs = refs[4 : 4 + shares]
    window, joined, refs = refs[4 + shares], refs[5 + shares], refs[6 + shares :]
    block, me = lax.axis_index("cascade"), lax.axis_index("coil")
    coils, phases, readouts, rows, part = samples.shape[1:]
    count = rows // 2
    share = count // shares

    if direct:
        waits = {}
        maps, samples = maps.at[block], samples.at[block]
    else:
        sems = refs[-1]
        sources = (tables, images[0].at[block], maps.at[block], mask, samples.at[block])
        names = ("tables", "image", "maps", "mask", "samples")
        waits = {}
        for k, (name, source) in enumerate(zip(names, sources)):
            waits[name] = pltpu.make_async_copy(source, refs[k], sems.at[k])
        for name in names:
            waits[name].start()
        tables, image, maps, mask, samples = refs[:5]

    def wait(name):
        if name in waits:
            waits.pop(name).wait()

    wait("tables")
    wait("image")
    if pieces > 1:
        image = joined
        for k in range(pieces):
            to = pl.multiple_of(lax.rem(me + (pieces - k), pieces) * 2 * share, 2 * share)
            joined[:, :, pl.ds(to, 2 * share)] = images[k][...]

    def apart(values):
        return dot(tables[4, :rows, :rows], values)

    def lane(n):
        return slice(n * part, (n + 1) * part)

    def band(n):
        return slice(n * count, (n + 1) * count)

    places = [(r, p) for r in range(readouts) for p in range(phases)]
    image_now = apart(jnp.concatenate([image[p, r] for r, p in places], 1))
    wait("maps")
    maps_now = apart(
        jnp.concatenate([maps[coil, r] for r in range(readouts) for coil in range(coils)], 1)
    )

    def map_parts(r, coil):
        where = lane(r * coils + coil)
        return maps_now[:count, where], maps_now[count:, where]

    slabs = [(r, coil, p) for r in range(readouts) for coil in range(coils) for p in range(phases)]
    real_sum = {place: 0.0 for place in places}
    imag_sum = {place: 0.0 for place in places}
    for begin in range(0, len(slabs), batch):
        group = slabs[begin : begin + batch]
        every = range(len(group))
        fields = []
        for r, coil, p in group:
            map_real, map_imag = map_parts(r, coil)
            where = lane(places.index((r, p)))
            real, imag = image_now[:count, where], image_now[count:, where]
            fields.append(
                jnp.concatenate(
                    [
                        (map_real * real - map_imag * imag).astype(BF16),
                        (map_real * imag + map_imag * real).astype(BF16),
                    ],
                    1,
                )
            )
        half = dot(jnp.concatenate(fields, 0), tables[0, : 2 * part, : 2 * part]).astype(BF16)
        stacked = jnp.concatenate(
            [jnp.concatenate([half[band(n), :part], half[band(n), part:]], 0) for n in every], 1
        )
        spectrum = dot(tables[1, :rows, :rows], stacked)
        wait("mask")
        wait("samples")
        measured = apart(jnp.concatenate([samples[coil, p, r] for r, coil, p in group], 1))
        acquired = jnp.concatenate([mask[coil, p] for r, coil, p in group], 1) != 0
        mixed = jnp.concatenate(
            [
                jnp.where(acquired, measured[:count], spectrum[:count]).astype(BF16),
                jnp.where(acquired, measured[count:], spectrum[count:]).astype(BF16),
            ],
            0,
        )
        back = dot(tables[2, :rows, :rows], mixed).astype(BF16)
        paired = jnp.concatenate(
            [jnp.concatenate([back[:count, lane(n)], back[count:, lane(n)]], 1) for n in every], 0
        )
        restored = dot(paired, tables[3, : 2 * part, : 2 * part])
        for n, (r, coil, p) in enumerate(group):
            map_real, map_imag = map_parts(r, coil)
            real, imag = restored[band(n), :part], restored[band(n), part:]
            real_sum[r, p] = real_sum[r, p] + (map_real * real + map_imag * imag)
            imag_sum[r, p] = imag_sum[r, p] + (map_real * imag - map_imag * real)

    blocks = []
    for r in range(readouts):
        summed = [
            v.astype(BF16) for p in range(phases) for v in (real_sum[r, p], imag_sum[r, p])
        ]
        blocks += [
            jnp.concatenate([v[k * share : (k + 1) * share] for v in summed], 0)
            for k in range(shares)
        ]
    width = phases * 2 * share
    ordered = dot(tables[5, :width, :width], jnp.concatenate(blocks, 1)).astype(BF16)
    border = jnp.zeros((edge, part), BF16)
    for r in range(readouts):
        window[r, 0:edge] = border
        window[r, edge + shares * width : 2 * edge + shares * width] = border
        for k in range(shares):
            window[r, edge + k * width : edge + (k + 1) * width] = ordered[:, lane(r * shares + k)]
    for k in range(shares):
        begin = pl.multiple_of(lax.rem(me + k, shares) * width, width)
        outs[k][...] = window[:, pl.ds(begin, width + 2 * edge)]


def consistency(images, maps, samples, mask, shares):
    blocks, coils, phases, readouts, rows, part = samples.shape
    lines = rows // 2
    share_rows = rows // shares
    edge = HALO * phases * 2
    tables = bf16(consistency_tables(lines, part, phases, lines // shares))
    pieces = len(images)
    direct = pieces > 1
    width = phases * share_rows + 2 * edge
    body = functools.partial(
        consistency_kernel, pieces=pieces, shares=shares, edge=edge, batch=BATCH, direct=direct
    )
    image_shape = (phases, readouts, rows, part)
    buffers = [
        pltpu.VMEM(tables.shape, BF16),
        pltpu.VMEM(image_shape, BF16),
        pltpu.VMEM((coils, readouts, rows, part), BF16),
        pltpu.VMEM((coils, phases, lines, part), jnp.int32),
        pltpu.VMEM((coils, phases, readouts, rows, part), BF16),
        pltpu.SemaphoreType.DMA((5,)),
    ]
    return pl.pallas_call(
        body,
        in_specs=[pl.BlockSpec(memory_space=pltpu.VMEM if direct else pl.ANY)] * (pieces + 4),
        out_specs=[pl.BlockSpec(memory_space=pltpu.VMEM)] * shares,
        scratch_shapes=[
            pltpu.VMEM((readouts, shares * phases * share_rows + 2 * edge, part), BF16),
            pltpu.VMEM(image_shape if direct else (16, part), BF16),
        ]
        + ([] if direct else buffers),
        out_shape=[jax.ShapeDtypeStruct((readouts, width, part), BF16)] * shares,
        compiler_params=pltpu.CompilerParams(
            vmem_limit_bytes=VMEM_LIMIT if direct else WIDE_LIMIT
        ),
        cost_estimate=pl.CostEstimate(
            flops=readouts * coils * phases * rows * part * rows * 20,
            bytes_accessed=4 * 1024 * 1024,
            transcendentals=0,
        ),
        name="consistency",
    )(*images, maps, samples, mask, tables)


def tap_rows(phases, parts):
    rows = []
    for row_shift in range(3):
        for tap in range(9):
            for phase in range(phases):
                for piece in range(parts):
                    rows.append(((9 * row_shift + tap) * parts + piece, phase))
        rows += [(-1, -1)] * (-(9 * phases * parts) % 16)
    return rows


@functools.lru_cache(maxsize=None)
def weight_tables(phases, channels):
    rows = tap_rows(phases, 2)
    spread = np.zeros((len(rows), 64))
    own_phase = np.zeros((len(rows), phases * channels))
    for index, (source, phase) in enumerate(rows):
        if source >= 0:
            spread[index, source] = 1.0
            own_phase[index, phase * channels : (phase + 1) * channels] = 1.0
    tiled = np.tile(np.eye(channels), (1, phases))
    phase_of = np.repeat(np.arange(phases), channels)
    time_masks = np.stack(
        [phase_of[None, :] - phase_of[:, None] == 2 * (k - 1) for k in range(3)]
    ).astype(np.float64)
    return spread, own_phase, tiled, time_masks


def weights_kernel(*refs, pieces):
    packs = refs[:pieces]
    spread, spread_t, own_phase, own_phase_t, tiled, tiled_t, time_masks = refs[pieces : pieces + 7]
    first_out, time_out, last_out = refs[pieces + 7 :]
    channels = tiled.shape[0]
    me = lax.axis_index("cascade")

    def transposed(block):
        return lax.dot_general(
            tiled_t[...], block, (((1,), (1,)), ((), ())), preferred_element_type=F32
        ).astype(BF16)

    for section in range(pieces):
        pick = lax.rem(me - section + pieces, pieces)
        pack = packs[0][...].astype(F32)
        for k in range(1, pieces):
            pack = jnp.where(pick == k, packs[k][...].astype(F32), pack)
        pack = pack.astype(BF16)
        time = 0.0
        for k in range(3):
            block = transposed(pack[k * channels : (k + 1) * channels])
            time = time + dot(block, tiled[...]) * time_masks[k].astype(F32)
        time_out[section] = time.astype(BF16)
        first = transposed(pack[3 * channels : 3 * channels + 64])
        first_out[section] = (dot(first, spread_t[...]) * own_phase_t[...].astype(F32)).astype(BF16)
        last = dot(spread[...], pack[3 * channels + 64 :]).astype(BF16)
        last_out[section] = (dot(last, tiled[...]) * own_phase[...].astype(F32)).astype(BF16)


def weight_matrices(packs, phases):
    sections = len(packs)
    channels = packs[0].shape[1]
    spread, own_phase, tiled, time_masks = weight_tables(phases, channels)
    tables = [
        bf16(t) for t in (spread, spread.T, own_phase, own_phase.T, tiled, tiled.T, time_masks)
    ]
    wide = phases * channels
    taps = spread.shape[0]
    shapes = [(wide, taps), (wide, wide), (taps, wide)]
    return pl.pallas_call(
        functools.partial(weights_kernel, pieces=sections),
        in_specs=[pl.BlockSpec(memory_space=pltpu.VMEM)] * (sections + len(tables)),
        out_specs=[pl.BlockSpec(memory_space=pltpu.VMEM)] * len(shapes),
        out_shape=[jax.ShapeDtypeStruct((sections,) + s, BF16) for s in shapes],
        compiler_params=pltpu.CompilerParams(vmem_limit_bytes=VMEM_LIMIT),
        cost_estimate=pl.CostEstimate(
            flops=sections * wide * wide * 1000, bytes_accessed=2 * 1024 * 1024, transcendentals=0
        ),
        name="weights",
    )(*packs, *tables)


def shifted(values, step):
    part = values.shape[1]
    lane = lax.broadcasted_iota(jnp.int32, values.shape, 1)
    if step > 0:
        return jnp.where(lane == 0, 0.0, pltpu.roll(values, 1, 1))
    return jnp.where(lane == part - 1, 0.0, pltpu.roll(values, part - 1, 1))


def denoise_kernel(*refs, phases, section, second):
    own, beside, first, time, last, *refs = refs
    if second:
        before, apart, out, taps, sums = refs
    else:
        sums, taps = refs
    readouts, span, part = own.shape
    cell = 2 * phases
    lines = span // cell
    group = taps.shape[2]
    used = 9 * cell
    readout_no, coil_no = lax.axis_index("readout"), lax.axis_index("coil")
    upward = lax.rem(readout_no, 2) == (1 if second else 0)
    there = jnp.where(upward, readout_no < lax.axis_size("readout") - 1, readout_no > 0)
    first_line = (coil_no > 0).astype(F32).astype(BF16)
    last_line = (coil_no < lax.axis_size("coil") - 1).astype(F32).astype(BF16)

    own_at = jnp.where(upward, 0, HALO)
    beside_at = jnp.where(upward, readouts, 0)
    slabs = [(own_at + k, own[k].astype(F32)) for k in range(readouts)]
    for k in range(HALO):
        value = jnp.where(upward, beside[k].astype(F32), beside[readouts - HALO + k].astype(F32))
        slabs.append((beside_at + k, jnp.where(there, value, 0.0)))
    filler = [jnp.zeros((group - used, part), F32)] if group > used else []
    for index, slab in slabs:
        views = [shifted(slab, 1), slab, shifted(slab, -1)]
        for line in range(1, lines - 1):
            around = [
                views[e][cell * (line + c - 1) : cell * (line + c)] for c in range(3) for e in range(3)
            ]
            taps[index, line - 1] = jnp.concatenate(around + filler, 0).astype(BF16)
    sums[...] = jnp.zeros_like(sums)

    def add_row(row, begun, count):
        start = row - 1 + own_at
        block = range(1, lines - 1)
        near = jnp.concatenate(
            [taps[pl.ds(start, 3), line - 1].reshape(3 * group, part) for line in block], 1
        )
        hidden = jnp.maximum(dot(first[section], near), 0.0).astype(BF16)
        mixed = jnp.maximum(hidden.astype(F32) + dot(time[section], hidden), 0.0).astype(BF16)
        edge = (len(block) - 1) * part
        mixed = jnp.concatenate(
            [mixed[:, :part] * first_line, mixed[:, part:edge], mixed[:, edge:] * last_line], 1
        )
        chosen = pl.ds(pl.multiple_of(begun * group, 16), count * group)
        result = dot(last[section, chosen], mixed)
        for a in range(count):
            target = row + 1 - begun - a
            for e in range(3):
                for line in range(lines):
                    terms = []
                    for c in range(3):
                        source = line + c - 2
                        if 0 <= source < len(block):
                            at = a * group + (3 * c + e) * cell
                            terms.append(
                                result[at : at + cell, source * part : (source + 1) * part]
                            )
                    sums[e, target, line * cell : (line + 1) * cell] += sum(terms[1:], terms[0])

    @pl.when(there)
    def _():
        add_row(jnp.where(upward, readouts, -1), jnp.where(upward, 2, 0), 1)

    add_row(jnp.where(upward, readouts - 1, 0), jnp.where(upward, 1, 0), 2)
    if not second:
        for row in range(1, readouts - 1):
            add_row(row, 0, 3)
        return

    body = slice(HALO * cell, span - HALO * cell)
    finals = []
    for r in range(readouts):
        left, here, right = [sums[e, r, body] + before[e, r, body] for e in range(3)]
        value = own[r, body].astype(F32) + here + shifted(left, 1) + shifted(right, -1)
        finals.append(value.astype(BF16))
    ordered = dot(apart[...], jnp.concatenate(finals, 1)).astype(BF16)
    height = out.shape[2]
    for p in range(phases):
        for r in range(readouts):
            out[p, r] = ordered[p * height : (p + 1) * height, r * part : (r + 1) * part]


def denoise(own, beside, matrices, section, phases, before=None):
    readouts, span, part = own.shape
    cell = 2 * phases
    lines = span // cell
    share = lines - 2 * HALO
    group = matrices[0].shape[2] // 3
    second = before is not None
    operands = [own, beside, *matrices]
    sums_shape = (3, readouts, span, part)
    scratch = [pltpu.VMEM((readouts + HALO, lines - 2, group, part), BF16)]
    result = jax.ShapeDtypeStruct(sums_shape, F32)
    if second:
        operands += [before, bf16(phase_inside(phases, share).T)]
        scratch.append(pltpu.VMEM(sums_shape, F32))
        result = jax.ShapeDtypeStruct((phases, readouts, 2 * share, part), BF16)
    return pl.pallas_call(
        functools.partial(denoise_kernel, phases=phases, section=section, second=second),
        in_specs=[pl.BlockSpec(memory_space=pltpu.VMEM)] * len(operands),
        out_specs=pl.BlockSpec(memory_space=pltpu.VMEM),
        scratch_shapes=scratch,
        out_shape=result,
        compiler_params=pltpu.CompilerParams(vmem_limit_bytes=VMEM_LIMIT),
        cost_estimate=pl.CostEstimate(
            flops=6 * readouts * lines * part * 256 * 256,
            bytes_accessed=2 * 1024 * 1024,
            transcendentals=0,
        ),
        name="denoise",
    )(*operands)


def rotation(count, step):
    return [(i, (i + step) % count) for i in range(count)]


def swaps(count, first):
    pairs = [(i, i + 1) for i in range(first, count - 1, 2)]
    return pairs + [(target, source) for source, target in pairs]


def exchanged(values, axis, count):
    arrived = {0: values[0]}
    for k in sorted(range(1, count), key=lambda k: abs(k - count / 2)):
        arrived[k] = lax.ppermute(values[k], axis, rotation(count, k))
    return [arrived[k] for k in range(count)]


def per_device(initial, coil_maps, kspace, sampled, first_w, time_w, last_w):
    section_no = lax.axis_index("cascade")
    sections = lax.axis_size("cascade")
    shares = lax.axis_size("coil")
    readout_parts = lax.axis_size("readout")
    phases = kspace.shape[2]
    part = kspace.shape[-1]
    channels = first_w.shape[-1]

    def rows_of(array):
        return array.reshape(array.shape[:-3] + (2 * array.shape[-3], part))

    def padded(block):
        return jnp.pad(block, ((0, -block.shape[0] % 64), (0, 0)))

    initial, coil_maps, kspace = rows_of(initial), rows_of(coil_maps), rows_of(kspace)
    images = [initial]
    matrices = None
    sent = []
    for section in range(sections):
        partial = consistency(images, coil_maps, kspace, sampled, shares)
        if matrices is None:
            partial, (first_w, time_w, last_w) = lax.optimization_barrier(
                (partial, (first_w, time_w, last_w))
            )
        parts = exchanged(partial, "coil", shares)
        if matrices is None:
            pack = jnp.concatenate(
                [
                    time_w[0].reshape(-1, channels),
                    padded(first_w[0].reshape(-1, channels)),
                    padded(jnp.swapaxes(last_w[0], 1, 2).reshape(-1, channels)),
                ],
                0,
            )
            packs = exchanged([pack] * sections, "cascade", sections)
            matrices = weight_matrices(packs, phases)
            parts, matrices = lax.optimization_barrier((parts, matrices))
        else:
            parts, sent[-1] = lax.optimization_barrier((parts, sent[-1]))
        combined = sum(p.astype(F32) for p in parts).astype(BF16)
        even = lax.ppermute(combined, "readout", swaps(readout_parts, 0))
        odd = lax.ppermute(combined, "readout", swaps(readout_parts, 1))
        reached = denoise(combined, even, matrices, section, phases)
        output = denoise(combined, odd, matrices, section, phases, reached)
        if section < sections - 1:
            images = exchanged([output] * shares, "coil", shares)
        sent.append(exchanged([output] * sections, "cascade", sections))

    arrived = []
    for block in range(sections):
        value = None
        for section in range(sections):
            k = (section - block) % sections
            piece = sent[section][k]
            value = piece if value is None else jnp.where(section_no == section, piece, value)
        arrived.append(value)
    result = jnp.stack(arrived)[None]
    return result.reshape(result.shape[:-2] + (result.shape[-2] // 2, 2, part))


def solution(mesh):
    in_specs = (
        P(None, None, "readout", None, None, None),
        P(None, "coil", "readout", None, None, None),
        P(None, "coil", None, "readout", None, None, None),
        P("coil", None, None, None),
        P("cascade", None, None, None),
        P("cascade", None, None, None),
        P("cascade", None, None, None),
    )
    out_specs = P("cascade", None, None, "readout", "coil", None, None)
    return jax.shard_map(
        per_device, mesh=mesh, in_specs=in_specs, out_specs=out_specs, check_vma=False
    )
```

```python
import functools

import jax
import jax.numpy as jnp
import numpy as np
from jax import lax
from jax.experimental import pallas as pl
from jax.experimental.pallas import tpu as pltpu
from jax.sharding import PartitionSpec as P

F32 = jnp.float32
BF16 = jnp.bfloat16
HALO = 2
BATCH = 16
VMEM_LIMIT = 30 * 1024 * 1024


def fourier_pair(length):
    positions = np.arange(length, dtype=np.int64)
    angles = (positions[:, None] * positions[None, :] % length) * (2.0 * np.pi / length)
    factor = 1.0 / np.sqrt(float(length))
    return np.cos(angles) * factor, np.sin(angles) * factor


def bf16(values):
    return jnp.asarray(values.astype(jnp.bfloat16))


def column_matrix(length, direction):
    cosine, sine = fourier_pair(length)
    return np.block([[cosine, direction * sine], [-direction * sine, cosine]])


def parts_apart(length):
    rows = np.arange(2 * length).reshape(length, 2).T.reshape(-1)
    return np.eye(2 * length)[rows]


@functools.lru_cache(maxsize=None)
def consistency_tables(line_total, part_total, phases, share):
    tables = [
        column_matrix(part_total, -1.0),
        column_matrix(line_total, -1.0).T,
        column_matrix(line_total, 1.0).T,
        column_matrix(part_total, 1.0),
        parts_apart(line_total),
        line_major(phases, share),
    ]
    size = max(max(t.shape) for t in tables)
    stacked = np.zeros((len(tables), size, size))
    for index, table in enumerate(tables):
        stacked[index, : table.shape[0], : table.shape[1]] = table
    return stacked


def line_major(phases, share):
    rows = np.arange(phases * 2 * share).reshape(phases * 2, share).T.reshape(-1)
    return np.eye(phases * 2 * share)[rows]


def phase_inside(phases, share):
    rows = np.arange(phases * share * 2).reshape(phases, share, 2).transpose(1, 0, 2).reshape(-1)
    return np.eye(phases * share * 2)[rows]


def dot(left, right):
    return jnp.dot(left, right, preferred_element_type=F32)


def consistency_kernel(*refs, pieces, shares, edge, batch, direct, chosen):
    images, refs = refs[:pieces], refs[pieces:]
    maps, samples, mask, tables = refs[:4]
    outs = refs[4 : 4 + shares]
    window, joined, refs = refs[4 + shares], refs[5 + shares], refs[6 + shares :]
    block, me = lax.axis_index("cascade"), lax.axis_index("coil")
    coils, phases, _, rows, part = samples.shape[1:]
    readouts = len(chosen)
    count = rows // 2
    share = count // shares

    if direct:
        waits = {}
        maps, samples = maps.at[block], samples.at[block]
    else:
        sems = refs[-1]
        sources = (tables, images[0].at[block], maps.at[block], mask, samples.at[block])
        names = ("tables", "image", "maps", "mask", "samples")
        waits = {}
        for k, (name, source) in enumerate(zip(names, sources)):
            waits[name] = pltpu.make_async_copy(source, refs[k], sems.at[k])
        for name in names:
            waits[name].start()
        tables, image, maps, mask, samples = refs[:5]

    def wait(name):
        if name in waits:
            waits.pop(name).wait()

    wait("tables")
    wait("image")
    if pieces > 1:
        image = joined
        for k in range(pieces):
            to = pl.multiple_of(lax.rem(me + (pieces - k), pieces) * 2 * share, 2 * share)
            joined[:, :, pl.ds(to, 2 * share)] = images[k][...]

    def apart(values):
        return dot(tables[4, :rows, :rows], values)

    def lane(n):
        return slice(n * part, (n + 1) * part)

    def band(n):
        return slice(n * count, (n + 1) * count)

    places = [(r, p) for r in range(readouts) for p in range(phases)]
    image_now = apart(jnp.concatenate([image[p, r] for r, p in places], 1))
    wait("maps")
    maps_now = apart(
        jnp.concatenate([maps[coil, r] for r in chosen for coil in range(coils)], 1)
    )

    def map_parts(r, coil):
        where = lane(r * coils + coil)
        return maps_now[:count, where], maps_now[count:, where]

    slabs = [(r, coil, p) for r in range(readouts) for coil in range(coils) for p in range(phases)]
    real_sum = {place: 0.0 for place in places}
    imag_sum = {place: 0.0 for place in places}
    for begin in range(0, len(slabs), batch):
        group = slabs[begin : begin + batch]
        every = range(len(group))
        fields = []
        for r, coil, p in group:
            map_real, map_imag = map_parts(r, coil)
            where = lane(places.index((r, p)))
            real, imag = image_now[:count, where], image_now[count:, where]
            fields.append(
                jnp.concatenate(
                    [
                        (map_real * real - map_imag * imag).astype(BF16),
                        (map_real * imag + map_imag * real).astype(BF16),
                    ],
                    1,
                )
            )
        half = dot(jnp.concatenate(fields, 0), tables[0, : 2 * part, : 2 * part]).astype(BF16)
        stacked = jnp.concatenate(
            [jnp.concatenate([half[band(n), :part], half[band(n), part:]], 0) for n in every], 1
        )
        spectrum = dot(tables[1, :rows, :rows], stacked)
        wait("mask")
        wait("samples")
        measured = apart(
            jnp.concatenate([samples[coil, p, chosen[r]] for r, coil, p in group], 1)
        )
        acquired = jnp.concatenate([mask[coil, p] for r, coil, p in group], 1) != 0
        mixed = jnp.concatenate(
            [
                jnp.where(acquired, measured[:count], spectrum[:count]).astype(BF16),
                jnp.where(acquired, measured[count:], spectrum[count:]).astype(BF16),
            ],
            0,
        )
        back = dot(tables[2, :rows, :rows], mixed).astype(BF16)
        paired = jnp.concatenate(
            [jnp.concatenate([back[:count, lane(n)], back[count:, lane(n)]], 1) for n in every], 0
        )
        restored = dot(paired, tables[3, : 2 * part, : 2 * part])
        for n, (r, coil, p) in enumerate(group):
            map_real, map_imag = map_parts(r, coil)
            real, imag = restored[band(n), :part], restored[band(n), part:]
            real_sum[r, p] = real_sum[r, p] + (map_real * real + map_imag * imag)
            imag_sum[r, p] = imag_sum[r, p] + (map_real * imag - map_imag * real)

    blocks = []
    for r in range(readouts):
        summed = [
            v.astype(BF16) for p in range(phases) for v in (real_sum[r, p], imag_sum[r, p])
        ]
        blocks += [
            jnp.concatenate([v[k * share : (k + 1) * share] for v in summed], 0)
            for k in range(shares)
        ]
    width = phases * 2 * share
    ordered = dot(tables[5, :width, :width], jnp.concatenate(blocks, 1)).astype(BF16)
    border = jnp.zeros((edge, part), BF16)
    for r in range(readouts):
        window[r, 0:edge] = border
        window[r, edge + shares * width : 2 * edge + shares * width] = border
        for k in range(shares):
            window[r, edge + k * width : edge + (k + 1) * width] = ordered[:, lane(r * shares + k)]
    for k in range(shares):
        begin = pl.multiple_of(lax.rem(me + k, shares) * width, width)
        outs[k][...] = window[:, pl.ds(begin, width + 2 * edge)]


def consistency(images, maps, samples, mask, shares, chosen):
    blocks, coils, phases, every, rows, part = samples.shape
    readouts = len(chosen)
    lines = rows // 2
    share_rows = rows // shares
    edge = HALO * phases * 2
    tables = bf16(consistency_tables(lines, part, phases, lines // shares))
    pieces = len(images)
    direct = pieces > 1
    width = phases * share_rows + 2 * edge
    body = functools.partial(
        consistency_kernel, pieces=pieces, shares=shares, edge=edge, batch=BATCH, direct=direct, chosen=chosen
    )
    image_shape = (phases, readouts, rows, part)
    buffers = [
        pltpu.VMEM(tables.shape, BF16),
        pltpu.VMEM(image_shape, BF16),
        pltpu.VMEM((coils, every, rows, part), BF16),
        pltpu.VMEM((coils, phases, lines, part), jnp.int32),
        pltpu.VMEM((coils, phases, every, rows, part), BF16),
        pltpu.SemaphoreType.DMA((5,)),
    ]
    return pl.pallas_call(
        body,
        in_specs=[pl.BlockSpec(memory_space=pltpu.VMEM if direct else pl.ANY)] * (pieces + 4),
        out_specs=[pl.BlockSpec(memory_space=pltpu.VMEM)] * shares,
        scratch_shapes=[
            pltpu.VMEM((readouts, shares * phases * share_rows + 2 * edge, part), BF16),
            pltpu.VMEM(image_shape if direct else (16, part), BF16),
        ]
        + ([] if direct else buffers),
        out_shape=[jax.ShapeDtypeStruct((readouts, width, part), BF16)] * shares,
        compiler_params=pltpu.CompilerParams(
            vmem_limit_bytes=VMEM_LIMIT
        ),
        cost_estimate=pl.CostEstimate(
            flops=readouts * coils * phases * rows * part * rows * 20,
            bytes_accessed=4 * 1024 * 1024,
            transcendentals=0,
        ),
        name="consistency",
    )(*[x if direct else pltpu.with_memory_space_constraint(x, pltpu.HBM) for x in (*images, maps, samples, mask, tables)])


def tap_rows(phases, parts):
    rows = []
    for row_shift in range(3):
        for tap in range(9):
            for phase in range(phases):
                for piece in range(parts):
                    rows.append(((9 * row_shift + tap) * parts + piece, phase))
        rows += [(-1, -1)] * (-(9 * phases * parts) % 16)
    return rows


@functools.lru_cache(maxsize=None)
def weight_tables(phases, channels):
    rows = tap_rows(phases, 2)
    spread = np.zeros((len(rows), 64))
    own_phase = np.zeros((len(rows), phases * channels))
    for index, (source, phase) in enumerate(rows):
        if source >= 0:
            spread[index, source] = 1.0
            own_phase[index, phase * channels : (phase + 1) * channels] = 1.0
    tiled = np.tile(np.eye(channels), (1, phases))
    phase_of = np.repeat(np.arange(phases), channels)
    time_masks = np.stack(
        [phase_of[None, :] - phase_of[:, None] == 2 * (k - 1) for k in range(3)]
    ).astype(np.float64)
    return spread, own_phase, tiled, time_masks


def weights_kernel(*refs, pieces):
    packs = refs[:pieces]
    spread, spread_t, own_phase, own_phase_t, tiled, tiled_t, time_masks = refs[pieces : pieces + 7]
    first_out, time_out, last_out = refs[pieces + 7 :]
    channels = tiled.shape[0]
    me = lax.axis_index("cascade")

    def transposed(block):
        return lax.dot_general(
            tiled_t[...], block, (((1,), (1,)), ((), ())), preferred_element_type=F32
        ).astype(BF16)

    for section in range(pieces):
        pick = lax.rem(me - section + pieces, pieces)
        pack = packs[0][...].astype(F32)
        for k in range(1, pieces):
            pack = jnp.where(pick == k, packs[k][...].astype(F32), pack)
        pack = pack.astype(BF16)
        time = 0.0
        for k in range(3):
            block = transposed(pack[k * channels : (k + 1) * channels])
            time = time + dot(block, tiled[...]) * time_masks[k].astype(F32)
        time_out[section] = time.astype(BF16)
        first = transposed(pack[3 * channels : 3 * channels + 64])
        first_out[section] = (dot(first, spread_t[...]) * own_phase_t[...].astype(F32)).astype(BF16)
        last = dot(spread[...], pack[3 * channels + 64 :]).astype(BF16)
        last_out[section] = (dot(last, tiled[...]) * own_phase[...].astype(F32)).astype(BF16)


def weight_matrices(packs, phases):
    sections = len(packs)
    channels = packs[0].shape[1]
    spread, own_phase, tiled, time_masks = weight_tables(phases, channels)
    tables = [
        bf16(t) for t in (spread, spread.T, own_phase, own_phase.T, tiled, tiled.T, time_masks)
    ]
    wide = phases * channels
    taps = spread.shape[0]
    shapes = [(wide, taps), (wide, wide), (taps, wide)]
    return pl.pallas_call(
        functools.partial(weights_kernel, pieces=sections),
        in_specs=[pl.BlockSpec(memory_space=pltpu.VMEM)] * (sections + len(tables)),
        out_specs=[pl.BlockSpec(memory_space=pltpu.VMEM)] * len(shapes),
        out_shape=[jax.ShapeDtypeStruct((sections,) + s, BF16) for s in shapes],
        compiler_params=pltpu.CompilerParams(vmem_limit_bytes=VMEM_LIMIT),
        cost_estimate=pl.CostEstimate(
            flops=sections * wide * wide * 1000, bytes_accessed=2 * 1024 * 1024, transcendentals=0
        ),
        name="weights",
    )(*packs, *tables)


def shifted(values, step):
    part = values.shape[1]
    lane = lax.broadcasted_iota(jnp.int32, values.shape, 1)
    if step > 0:
        return jnp.where(lane == 0, 0.0, pltpu.roll(values, 1, 1))
    return jnp.where(lane == part - 1, 0.0, pltpu.roll(values, part - 1, 1))


def denoise_kernel(*refs, phases, section, stage):
    refs = list(refs)
    own = refs.pop(0)
    beside = None if stage == "alone" else refs.pop(0)
    first, time, last = refs[:3]
    refs = refs[3:]
    before = None if stage == "alone" else refs.pop(0)
    if stage == "far":
        apart, *outs, taps, sums = refs
    else:
        sums, taps = refs
    readouts, span, part = own.shape
    cell = 2 * phases
    lines = span // cell
    group = taps.shape[2]
    used = 9 * cell
    readout_no, coil_no = lax.axis_index("readout"), lax.axis_index("coil")
    upward = lax.rem(readout_no, 2) == (0 if stage == "near" else 1)
    there = jnp.where(upward, readout_no < lax.axis_size("readout") - 1, readout_no > 0)
    first_line = (coil_no > 0).astype(F32).astype(BF16)
    last_line = (coil_no < lax.axis_size("coil") - 1).astype(F32).astype(BF16)
    own_at = jnp.where(upward, 0, HALO)
    beside_at = jnp.where(upward, readouts, 0)

    def fill_taps():
        slabs = [(own_at + k, own[k].astype(F32)) for k in range(readouts)]
        for k in range(HALO):
            value = jnp.zeros((span, part), F32)
            if beside is not None:
                low = beside[readouts - HALO + k].astype(F32)
                value = jnp.where(there, jnp.where(upward, beside[k].astype(F32), low), value)
            slabs.append((beside_at + k, value))
        filler = [jnp.zeros((group - used, part), F32)] if group > used else []
        for index, slab in slabs:
            views = [shifted(slab, 1), slab, shifted(slab, -1)]
            for line in range(1, lines - 1):
                around = [
                    views[e][cell * (line + c - 1) : cell * (line + c)]
                    for c in range(3)
                    for e in range(3)
                ]
                taps[index, line - 1] = jnp.concatenate(around + filler, 0).astype(BF16)

    def add_row(row, begun, count):
        start = row - 1 + own_at
        block = range(1, lines - 1)
        near = jnp.concatenate(
            [taps[pl.ds(start, 3), line - 1].reshape(3 * group, part) for line in block], 1
        )
        hidden = jnp.maximum(dot(first[section], near), 0.0).astype(BF16)
        mixed = jnp.maximum(hidden.astype(F32) + dot(time[section], hidden), 0.0).astype(BF16)
        edge = (len(block) - 1) * part
        mixed = jnp.concatenate(
            [mixed[:, :part] * first_line, mixed[:, part:edge], mixed[:, edge:] * last_line], 1
        )
        chosen = pl.ds(pl.multiple_of(begun * group, 16), count * group)
        result = dot(last[section, chosen], mixed)
        for a in range(count):
            target = row + 1 - begun - a
            for e in range(3):
                for line in range(lines):
                    terms = []
                    for c in range(3):
                        source = line + c - 2
                        if 0 <= source < len(block):
                            at = a * group + (3 * c + e) * cell
                            terms.append(
                                result[at : at + cell, source * part : (source + 1) * part]
                            )
                    sums[e, target, line * cell : (line + 1) * cell] += sum(terms[1:], terms[0])

    def add_outer():
        add_row(jnp.where(upward, readouts, -1), jnp.where(upward, 2, 0), 1)

    def add_inner():
        add_row(jnp.where(upward, readouts - 1, 0), jnp.where(upward, 1, 0), 2)

    sums[...] = jnp.zeros_like(sums) if before is None else before[...]
    if stage == "near":
        fill_taps()
        pl.when(there)(add_outer)
        add_inner()
        for row in range(1, readouts - 1):
            add_row(row, 0, 3)
        return

    @pl.when(there if stage == "far" else jnp.logical_not(there))
    def _():
        fill_taps()
        if stage == "far":
            add_outer()
        add_inner()

    if stage == "alone":
        return
    body = slice(HALO * cell, span - HALO * cell)
    finals = []
    for r in range(readouts):
        left, here, right = [sums[e, r, body] for e in range(3)]
        value = own[r, body].astype(F32) + here + shifted(left, 1) + shifted(right, -1)
        finals.append(value.astype(BF16))
    ordered = dot(apart[...], jnp.concatenate(finals, 1)).astype(BF16)
    height = outs[0].shape[2]
    for p in range(phases):
        for r in range(readouts):
            piece = ordered[p * height : (p + 1) * height, r * part : (r + 1) * part]
            outs[0][p, r] = piece
            if len(outs) > 1:
                outs[1 + r][p, 0] = piece


def denoise(stage, own, matrices, section, phases, beside=None, before=None, split=False):
    readouts, span, part = own.shape
    cell = 2 * phases
    lines = span // cell
    share = lines - 2 * HALO
    group = matrices[0].shape[2] // 3
    operands = [own] + [beside] * (stage != "alone") + list(matrices) + [before] * (stage != "alone")
    sums_shape = (3, readouts, span, part)
    scratch = [pltpu.VMEM((readouts + HALO, lines - 2, group, part), BF16)]
    result = [jax.ShapeDtypeStruct(sums_shape, F32)]
    if stage == "far":
        operands.append(bf16(phase_inside(phases, share).T))
        scratch.append(pltpu.VMEM(sums_shape, F32))
        result = [jax.ShapeDtypeStruct((phases, readouts, 2 * share, part), BF16)]
        if split:
            result += [jax.ShapeDtypeStruct((phases, 1, 2 * share, part), BF16)] * readouts
    return pl.pallas_call(
        functools.partial(denoise_kernel, phases=phases, section=section, stage=stage),
        in_specs=[pl.BlockSpec(memory_space=pltpu.VMEM)] * len(operands),
        out_specs=[pl.BlockSpec(memory_space=pltpu.VMEM)] * len(result),
        scratch_shapes=scratch,
        out_shape=result,
        compiler_params=pltpu.CompilerParams(vmem_limit_bytes=VMEM_LIMIT),
        cost_estimate=pl.CostEstimate(
            flops=(1 if stage == "alone" else 6) * readouts * lines * part * 256 * 256,
            bytes_accessed=2 * 1024 * 1024,
            transcendentals=0,
        ),
        name="denoise_" + stage,
    )(*operands)


def rotation(count, step):
    return [(i, (i + step) % count) for i in range(count)]


def swaps(count, first):
    pairs = [(i, (i + 1) % count) for i in range(first, count, 2)]
    return pairs + [(target, source) for source, target in pairs]


def exchanged(values, axis, count):
    arrived = {0: values[0]}
    for k in sorted(range(1, count), key=lambda k: abs(k - count / 2)):
        arrived[k] = lax.ppermute(values[k], axis, rotation(count, k))
    return [arrived[k] for k in range(count)]


def per_device(initial, coil_maps, kspace, sampled, first_w, time_w, last_w):
    section_no = lax.axis_index("cascade")
    sections = lax.axis_size("cascade")
    shares = lax.axis_size("coil")
    readout_parts = lax.axis_size("readout")
    phases = kspace.shape[2]
    part = kspace.shape[-1]
    channels = first_w.shape[-1]

    def rows_of(array):
        return array.reshape(array.shape[:-3] + (2 * array.shape[-3], part))

    def padded(block):
        return jnp.pad(block, ((0, -block.shape[0] % 64), (0, 0)))

    initial, coil_maps, kspace = rows_of(initial), rows_of(coil_maps), rows_of(kspace)
    readouts = kspace.shape[3]
    images = [[initial]]
    matrices = None
    sent = []
    for section in range(sections):
        if section == 0:
            choices = [tuple(range(readouts))]
        else:
            choices = [(r,) for r in range(readouts)]
        parts = []
        for image, chosen in zip(images, choices):
            partial = consistency(image, coil_maps, kspace, sampled, shares, chosen)
            if matrices is None:
                partial, (first_w, time_w, last_w) = lax.optimization_barrier(
                    (partial, (first_w, time_w, last_w))
                )
            if section > 0 and chosen[-1] == readouts - 1:
                partial, waiting = lax.optimization_barrier((partial, waiting))
                sent.append(exchanged([waiting] * sections, "cascade", sections))
            parts.append(exchanged(partial, "coil", shares))
        if matrices is None:
            pack = jnp.concatenate(
                [
                    time_w[0].reshape(-1, channels),
                    padded(first_w[0].reshape(-1, channels)),
                    padded(jnp.swapaxes(last_w[0], 1, 2).reshape(-1, channels)),
                ],
                0,
            )
            packs = exchanged([pack] * sections, "cascade", sections)
            matrices = weight_matrices(packs, phases)
            parts, matrices = lax.optimization_barrier((parts, matrices))
        else:
            parts, sent[-1] = lax.optimization_barrier((parts, sent[-1]))
        combined = jnp.concatenate(
            [sum(p.astype(F32) for p in pieces).astype(BF16) for pieces in parts], 0
        )
        even = lax.ppermute(combined, "readout", swaps(readout_parts, 0))
        odd = lax.ppermute(combined, "readout", swaps(readout_parts, 1))
        (sums,) = denoise("alone", combined, matrices, section, phases)
        (sums,) = denoise("near", combined, matrices, section, phases, even, sums)
        more = section < sections - 1
        output, *split = denoise("far", combined, matrices, section, phases, odd, sums, more)
        images = [exchanged([value] * shares, "coil", shares) for value in split]
        if more:
            waiting = output
        else:
            sent.append(exchanged([output] * sections, "cascade", sections))

    arrived = []
    for block in range(sections):
        value = None
        for section in range(sections):
            k = (section - block) % sections
            piece = sent[section][k]
            value = piece if value is None else jnp.where(section_no == section, piece, value)
        arrived.append(value)
    result = jnp.stack(arrived)[None]
    return result.reshape(result.shape[:-2] + (result.shape[-2] // 2, 2, part))


def solution(mesh):
    in_specs = (
        P(None, None, "readout", None, None, None),
        P(None, "coil", "readout", None, None, None),
        P(None, "coil", None, "readout", None, None, None),
        P("coil", None, None, None),
        P("cascade", None, None, None),
        P("cascade", None, None, None),
        P("cascade", None, None, None),
    )
    out_specs = P("cascade", None, None, "readout", "coil", None, None)
    return jax.shard_map(
        per_device, mesh=mesh, in_specs=in_specs, out_specs=out_specs, check_vma=False
    )
```

```python
import functools

import jax
import jax.numpy as jnp
import numpy as np
from jax import lax
from jax.experimental import pallas as pl
from jax.experimental.pallas import tpu as pltpu
from jax.sharding import PartitionSpec as P

F32 = jnp.float32
BF16 = jnp.bfloat16
HALO = 2
BATCH = 16
VMEM_LIMIT = 30 * 1024 * 1024


def fourier_pair(length):
    positions = np.arange(length, dtype=np.int64)
    angles = (positions[:, None] * positions[None, :] % length) * (2.0 * np.pi / length)
    factor = 1.0 / np.sqrt(float(length))
    return np.cos(angles) * factor, np.sin(angles) * factor


def bf16(values):
    return jnp.asarray(values.astype(jnp.bfloat16))


def column_matrix(length, direction):
    cosine, sine = fourier_pair(length)
    return np.block([[cosine, direction * sine], [-direction * sine, cosine]])


def parts_apart(length):
    rows = np.arange(2 * length).reshape(length, 2).T.reshape(-1)
    return np.eye(2 * length)[rows]


@functools.lru_cache(maxsize=None)
def consistency_tables(line_total, part_total, phases, share):
    tables = [
        column_matrix(part_total, -1.0),
        column_matrix(line_total, -1.0).T,
        column_matrix(line_total, 1.0).T,
        column_matrix(part_total, 1.0),
        parts_apart(line_total),
        line_major(phases, share),
    ]
    size = max(max(t.shape) for t in tables)
    stacked = np.zeros((len(tables), size, size))
    for index, table in enumerate(tables):
        stacked[index, : table.shape[0], : table.shape[1]] = table
    return stacked


def line_major(phases, share):
    rows = np.arange(phases * 2 * share).reshape(phases * 2, share).T.reshape(-1)
    return np.eye(phases * 2 * share)[rows]


def phase_inside(phases, share):
    rows = np.arange(phases * share * 2).reshape(phases, share, 2).transpose(1, 0, 2).reshape(-1)
    return np.eye(phases * share * 2)[rows]


def dot(left, right):
    return jnp.dot(left, right, preferred_element_type=F32)


def far_is_up():
    return lax.rem(lax.axis_index("readout"), 2) == 1


def side_count(side, readouts):
    return {"all": readouts, "near": readouts - 1, "far": 1}[side]


def side_rows(side, readouts):
    if side == "all":
        return list(range(readouts))
    up = far_is_up().astype(jnp.int32)
    if side == "far":
        return [up * (readouts - 1)]
    return [1 - up + k for k in range(readouts - 1)]


def consistency_kernel(*refs, pieces, shares, edge, batch, direct, side):
    images, refs = refs[:pieces], refs[pieces:]
    maps, samples, mask, tables = refs[:4]
    outs = refs[4 : 4 + shares]
    window, joined, refs = refs[4 + shares], refs[5 + shares], refs[6 + shares :]
    block, me = lax.axis_index("cascade"), lax.axis_index("coil")
    coils, phases, every, rows, part = samples.shape[1:]
    chosen = side_rows(side, every)
    readouts = len(chosen)
    count = rows // 2
    share = count // shares

    if direct:
        waits = {}
        maps, samples = maps.at[block], samples.at[block]
    else:
        sems = refs[-1]
        sources = (tables, images[0].at[block], maps.at[block], mask, samples.at[block])
        names = ("tables", "image", "maps", "mask", "samples")
        waits = {}
        for k, (name, source) in enumerate(zip(names, sources)):
            waits[name] = pltpu.make_async_copy(source, refs[k], sems.at[k])
        for name in names:
            waits[name].start()
        tables, image, maps, mask, samples = refs[:5]

    def wait(name):
        if name in waits:
            waits.pop(name).wait()

    wait("tables")
    wait("image")
    if pieces > 1:
        image = joined
        for k in range(pieces):
            to = pl.multiple_of(lax.rem(me + (pieces - k), pieces) * 2 * share, 2 * share)
            joined[:, :, pl.ds(to, 2 * share)] = images[k][...]

    def apart(values):
        return dot(tables[4, :rows, :rows], values)

    def lane(n):
        return slice(n * part, (n + 1) * part)

    def band(n):
        return slice(n * count, (n + 1) * count)

    places = [(r, p) for r in range(readouts) for p in range(phases)]
    image_now = apart(jnp.concatenate([image[p, r] for r, p in places], 1))
    wait("maps")
    maps_now = apart(
        jnp.concatenate([maps[coil, r] for r in chosen for coil in range(coils)], 1)
    )

    def map_parts(r, coil):
        where = lane(r * coils + coil)
        return maps_now[:count, where], maps_now[count:, where]

    slabs = [(r, coil, p) for r in range(readouts) for coil in range(coils) for p in range(phases)]
    real_sum = {place: 0.0 for place in places}
    imag_sum = {place: 0.0 for place in places}
    for begin in range(0, len(slabs), batch):
        group = slabs[begin : begin + batch]
        every = range(len(group))
        fields = []
        for r, coil, p in group:
            map_real, map_imag = map_parts(r, coil)
            where = lane(places.index((r, p)))
            real, imag = image_now[:count, where], image_now[count:, where]
            fields.append(
                jnp.concatenate(
                    [
                        (map_real * real - map_imag * imag).astype(BF16),
                        (map_real * imag + map_imag * real).astype(BF16),
                    ],
                    1,
                )
            )
        half = dot(jnp.concatenate(fields, 0), tables[0, : 2 * part, : 2 * part]).astype(BF16)
        stacked = jnp.concatenate(
            [jnp.concatenate([half[band(n), :part], half[band(n), part:]], 0) for n in every], 1
        )
        spectrum = dot(tables[1, :rows, :rows], stacked)
        wait("mask")
        wait("samples")
        measured = apart(
            jnp.concatenate([samples[coil, p, chosen[r]] for r, coil, p in group], 1)
        )
        acquired = jnp.concatenate([mask[coil, p] for r, coil, p in group], 1) != 0
        mixed = jnp.concatenate(
            [
                jnp.where(acquired, measured[:count], spectrum[:count]).astype(BF16),
                jnp.where(acquired, measured[count:], spectrum[count:]).astype(BF16),
            ],
            0,
        )
        back = dot(tables[2, :rows, :rows], mixed).astype(BF16)
        paired = jnp.concatenate(
            [jnp.concatenate([back[:count, lane(n)], back[count:, lane(n)]], 1) for n in every], 0
        )
        restored = dot(paired, tables[3, : 2 * part, : 2 * part])
        for n, (r, coil, p) in enumerate(group):
            map_real, map_imag = map_parts(r, coil)
            real, imag = restored[band(n), :part], restored[band(n), part:]
            real_sum[r, p] = real_sum[r, p] + (map_real * real + map_imag * imag)
            imag_sum[r, p] = imag_sum[r, p] + (map_real * imag - map_imag * real)

    blocks = []
    for r in range(readouts):
        summed = [
            v.astype(BF16) for p in range(phases) for v in (real_sum[r, p], imag_sum[r, p])
        ]
        blocks += [
            jnp.concatenate([v[k * share : (k + 1) * share] for v in summed], 0)
            for k in range(shares)
        ]
    width = phases * 2 * share
    ordered = dot(tables[5, :width, :width], jnp.concatenate(blocks, 1)).astype(BF16)
    border = jnp.zeros((edge, part), BF16)
    for r in range(readouts):
        window[r, 0:edge] = border
        window[r, edge + shares * width : 2 * edge + shares * width] = border
        for k in range(shares):
            window[r, edge + k * width : edge + (k + 1) * width] = ordered[:, lane(r * shares + k)]
    for k in range(shares):
        begin = pl.multiple_of(lax.rem(me + k, shares) * width, width)
        outs[k][...] = window[:, pl.ds(begin, width + 2 * edge)]


def consistency(images, maps, samples, mask, shares, side):
    blocks, coils, phases, every, rows, part = samples.shape
    readouts = side_count(side, every)
    lines = rows // 2
    share_rows = rows // shares
    edge = HALO * phases * 2
    tables = bf16(consistency_tables(lines, part, phases, lines // shares))
    pieces = len(images)
    direct = pieces > 1
    width = phases * share_rows + 2 * edge
    body = functools.partial(
        consistency_kernel, pieces=pieces, shares=shares, edge=edge, batch=BATCH, direct=direct, side=side
    )
    image_shape = (phases, readouts, rows, part)
    buffers = [
        pltpu.VMEM(tables.shape, BF16),
        pltpu.VMEM(image_shape, BF16),
        pltpu.VMEM((coils, every, rows, part), BF16),
        pltpu.VMEM((coils, phases, lines, part), jnp.int32),
        pltpu.VMEM((coils, phases, every, rows, part), BF16),
        pltpu.SemaphoreType.DMA((5,)),
    ]
    return pl.pallas_call(
        body,
        in_specs=[pl.BlockSpec(memory_space=pltpu.VMEM if direct else pl.ANY)] * (pieces + 4),
        out_specs=[pl.BlockSpec(memory_space=pltpu.VMEM)] * shares,
        scratch_shapes=[
            pltpu.VMEM((readouts, shares * phases * share_rows + 2 * edge, part), BF16),
            pltpu.VMEM(image_shape if direct else (16, part), BF16),
        ]
        + ([] if direct else buffers),
        out_shape=[jax.ShapeDtypeStruct((readouts, width, part), BF16)] * shares,
        compiler_params=pltpu.CompilerParams(
            vmem_limit_bytes=VMEM_LIMIT
        ),
        cost_estimate=pl.CostEstimate(
            flops=readouts * coils * phases * rows * part * rows * 20,
            bytes_accessed=4 * 1024 * 1024,
            transcendentals=0,
        ),
        name="consistency",
    )(*[x if direct else pltpu.with_memory_space_constraint(x, pltpu.HBM) for x in (*images, maps, samples, mask, tables)])


def tap_rows(phases, parts):
    rows = []
    for row_shift in range(3):
        for tap in range(9):
            for phase in range(phases):
                for piece in range(parts):
                    rows.append(((9 * row_shift + tap) * parts + piece, phase))
        rows += [(-1, -1)] * (-(9 * phases * parts) % 16)
    return rows


@functools.lru_cache(maxsize=None)
def weight_tables(phases, channels):
    rows = tap_rows(phases, 2)
    spread = np.zeros((len(rows), 64))
    own_phase = np.zeros((len(rows), phases * channels))
    for index, (source, phase) in enumerate(rows):
        if source >= 0:
            spread[index, source] = 1.0
            own_phase[index, phase * channels : (phase + 1) * channels] = 1.0
    tiled = np.tile(np.eye(channels), (1, phases))
    phase_of = np.repeat(np.arange(phases), channels)
    time_masks = np.stack(
        [phase_of[None, :] - phase_of[:, None] == 2 * (k - 1) for k in range(3)]
    ).astype(np.float64)
    return spread, own_phase, tiled, time_masks


def weights_kernel(*refs, pieces):
    packs = refs[:pieces]
    spread, spread_t, own_phase, own_phase_t, tiled, tiled_t, time_masks = refs[pieces : pieces + 7]
    first_out, time_out, last_out = refs[pieces + 7 :]
    channels = tiled.shape[0]
    me = lax.axis_index("cascade")

    def transposed(block):
        return lax.dot_general(
            tiled_t[...], block, (((1,), (1,)), ((), ())), preferred_element_type=F32
        ).astype(BF16)

    for section in range(pieces):
        pick = lax.rem(me - section + pieces, pieces)
        pack = packs[0][...].astype(F32)
        for k in range(1, pieces):
            pack = jnp.where(pick == k, packs[k][...].astype(F32), pack)
        pack = pack.astype(BF16)
        time = 0.0
        for k in range(3):
            block = transposed(pack[k * channels : (k + 1) * channels])
            time = time + dot(block, tiled[...]) * time_masks[k].astype(F32)
        time_out[section] = time.astype(BF16)
        first = transposed(pack[3 * channels : 3 * channels + 64])
        first_out[section] = (dot(first, spread_t[...]) * own_phase_t[...].astype(F32)).astype(BF16)
        last = dot(spread[...], pack[3 * channels + 64 :]).astype(BF16)
        last_out[section] = (dot(last, tiled[...]) * own_phase[...].astype(F32)).astype(BF16)


def weight_matrices(packs, phases):
    sections = len(packs)
    channels = packs[0].shape[1]
    spread, own_phase, tiled, time_masks = weight_tables(phases, channels)
    tables = [
        bf16(t) for t in (spread, spread.T, own_phase, own_phase.T, tiled, tiled.T, time_masks)
    ]
    wide = phases * channels
    taps = spread.shape[0]
    shapes = [(wide, taps), (wide, wide), (taps, wide)]
    return pl.pallas_call(
        functools.partial(weights_kernel, pieces=sections),
        in_specs=[pl.BlockSpec(memory_space=pltpu.VMEM)] * (sections + len(tables)),
        out_specs=[pl.BlockSpec(memory_space=pltpu.VMEM)] * len(shapes),
        out_shape=[jax.ShapeDtypeStruct((sections,) + s, BF16) for s in shapes],
        compiler_params=pltpu.CompilerParams(vmem_limit_bytes=VMEM_LIMIT),
        cost_estimate=pl.CostEstimate(
            flops=sections * wide * wide * 1000, bytes_accessed=2 * 1024 * 1024, transcendentals=0
        ),
        name="weights",
    )(*packs, *tables)


def shifted(values, step):
    part = values.shape[1]
    lane = lax.broadcasted_iota(jnp.int32, values.shape, 1)
    if step > 0:
        return jnp.where(lane == 0, 0.0, pltpu.roll(values, 1, 1))
    return jnp.where(lane == part - 1, 0.0, pltpu.roll(values, part - 1, 1))


def denoise_kernel(*refs, phases, section, stage):
    refs = list(refs)
    own = refs.pop(0)
    beside = None if stage == "alone" else refs.pop(0)
    first, time, last = refs[:3]
    refs = refs[3:]
    before = None if stage == "alone" else refs.pop(0)
    if stage == "far":
        apart, out, rest, taps, sums = refs
    elif stage == "last":
        apart, done, out, joint, taps, sums = refs
    elif stage == "end":
        apart, out, taps, sums = refs
    else:
        sums, taps = refs
    readouts, span, part = own.shape
    cell = 2 * phases
    lines = span // cell
    group = taps.shape[2]
    used = 9 * cell
    readout_no, coil_no = lax.axis_index("readout"), lax.axis_index("coil")
    upward = jnp.logical_not(far_is_up()) if stage == "near" else far_is_up()
    there = jnp.where(upward, readout_no < lax.axis_size("readout") - 1, readout_no > 0)
    first_line = (coil_no > 0).astype(F32).astype(BF16)
    last_line = (coil_no < lax.axis_size("coil") - 1).astype(F32).astype(BF16)

    def neighbour(k):
        if beside is None:
            return jnp.zeros((span, part), F32)
        low = beside[readouts - 1 - k].astype(F32)
        return jnp.where(there, jnp.where(upward, beside[k].astype(F32), low), 0.0)

    def inwards(k):
        return jnp.where(upward, own[readouts - 1 - k].astype(F32), own[k].astype(F32))

    def fill_taps(slabs):
        filler = [jnp.zeros((group - used, part), F32)] if group > used else []
        for k, slab in enumerate(slabs):
            index = jnp.where(upward, k, len(slabs) - 1 - k)
            views = [shifted(slab, 1), slab, shifted(slab, -1)]
            for line in range(1, lines - 1):
                around = [
                    views[e][cell * (line + c - 1) : cell * (line + c)]
                    for c in range(3)
                    for e in range(3)
                ]
                taps[index, line - 1] = jnp.concatenate(around + filler, 0).astype(BF16)

    def add_row(start, begun, count, target):
        block = range(1, lines - 1)
        near = jnp.concatenate(
            [taps[pl.ds(start, 3), line - 1].reshape(3 * group, part) for line in block], 1
        )
        hidden = jnp.maximum(dot(first[section], near), 0.0).astype(BF16)
        mixed = jnp.maximum(hidden.astype(F32) + dot(time[section], hidden), 0.0).astype(BF16)
        edge = (len(block) - 1) * part
        mixed = jnp.concatenate(
            [mixed[:, :part] * first_line, mixed[:, part:edge], mixed[:, edge:] * last_line], 1
        )
        chosen = pl.ds(pl.multiple_of(begun * group, 16), count * group)
        result = dot(last[section, chosen], mixed)
        for a in range(count):
            for e in range(3):
                for line in range(lines):
                    terms = []
                    for c in range(3):
                        source = line + c - 2
                        if 0 <= source < len(block):
                            at = a * group + (3 * c + e) * cell
                            terms.append(
                                result[at : at + cell, source * part : (source + 1) * part]
                            )
                    sums[e, target - a, line * cell : (line + 1) * cell] += sum(
                        terms[1:], terms[0]
                    )

    def add_outer(start, target):
        add_row(start, jnp.where(upward, 2, 0), 1, target)

    def add_inner(start):
        add_row(start, jnp.where(upward, 1, 0), 2, jnp.where(upward, readouts - 1, 1))

    def finished(rows):
        body = slice(HALO * cell, span - HALO * cell)
        finals = []
        for r, at in rows:
            left, here, right = [sums[e, at, body] for e in range(3)]
            value = own[r, body].astype(F32) + here + shifted(left, 1) + shifted(right, -1)
            finals.append(value.astype(BF16))
        ordered = dot(apart[...], jnp.concatenate(finals, 1)).astype(BF16)
        height = out.shape[2]
        for p in range(phases):
            for k in range(len(rows)):
                out[p, k] = ordered[p * height : (p + 1) * height, k * part : (k + 1) * part]

    sums[...] = jnp.zeros_like(sums) if before is None else before[...]
    if stage == "near":
        fill_taps([inwards(k) for k in reversed(range(readouts))] + [neighbour(0), neighbour(1)])
        pl.when(there)(lambda: add_outer(jnp.where(upward, readouts - 1, 0), jnp.where(upward, readouts - 1, 0)))
        add_inner(jnp.where(upward, readouts - 2, 1))
        for row in range(1, readouts - 1):
            add_row(row - 1 + jnp.where(upward, 0, HALO), 0, 3, row + 1)
    elif stage == "end":

        @pl.when(there)
        def _():
            fill_taps([inwards(1), inwards(0), neighbour(0), neighbour(1)])
            add_outer(jnp.where(upward, 1, 0), jnp.where(upward, readouts - 1, 0))
            add_inner(jnp.where(upward, 0, 1))

        finished([(row, row) for row in range(readouts)])
    elif stage == "last":

        @pl.when(there)
        def _():
            fill_taps([inwards(0), neighbour(0), neighbour(1)])
            add_outer(0, 0)

        (row,) = side_rows("far", readouts)
        finished([(row, 0)])
        joint[:, row] = out[:, 0]
        for k, near_row in enumerate(side_rows("near", readouts)):
            joint[:, near_row] = done[:, k]
    else:

        @pl.when(there if stage == "far" else jnp.logical_not(there))
        def _():
            fill_taps([inwards(1), inwards(0), neighbour(0)])
            add_inner(0)

        if stage == "far":
            finished([(row, row) for row in side_rows("near", readouts)])
            (row,) = side_rows("far", readouts)
            rest[:, 0] = sums[:, row]


def denoise(stage, own, matrices, section, phases, beside=None, before=None, done=None):
    readouts, span, part = own.shape
    cell = 2 * phases
    lines = span // cell
    share = lines - 2 * HALO
    group = matrices[0].shape[2] // 3
    operands = [own] + [beside] * (stage != "alone") + list(matrices) + [before] * (stage != "alone")
    sums_shape = (3, 1 if stage == "last" else readouts, span, part)
    depth = {"near": readouts + HALO, "end": 4}.get(stage, 3)
    scratch = [pltpu.VMEM((depth, lines - 2, group, part), BF16)]

    def image(count):
        return jax.ShapeDtypeStruct((phases, count, 2 * share, part), BF16)

    if stage in ("far", "last", "end"):
        operands.append(bf16(phase_inside(phases, share).T))
        scratch.append(pltpu.VMEM(sums_shape, F32))
    if stage == "far":
        result = [image(readouts - 1), jax.ShapeDtypeStruct((3, 1, span, part), F32)]
    elif stage == "last":
        operands.append(done)
        result = [image(1), image(readouts)]
    elif stage == "end":
        result = [image(readouts)]
    else:
        result = [jax.ShapeDtypeStruct(sums_shape, F32)]
    return pl.pallas_call(
        functools.partial(denoise_kernel, phases=phases, section=section, stage=stage),
        in_specs=[pl.BlockSpec(memory_space=pltpu.VMEM)] * len(operands),
        out_specs=[pl.BlockSpec(memory_space=pltpu.VMEM)] * len(result),
        scratch_shapes=scratch,
        out_shape=result,
        compiler_params=pltpu.CompilerParams(vmem_limit_bytes=VMEM_LIMIT),
        cost_estimate=pl.CostEstimate(
            flops={"alone": 1, "near": 6, "far": 3, "last": 3, "end": 6}[stage]
            * (readouts * lines * part * 256 * 256),
            bytes_accessed=2 * 1024 * 1024,
            transcendentals=0,
        ),
        name="denoise_" + stage,
    )(*operands)


def rotation(count, step):
    return [(i, (i + step) % count) for i in range(count)]


def swaps(count, first):
    pairs = [(i, (i + 1) % count) for i in range(first, count, 2)]
    return pairs + [(target, source) for source, target in pairs]


def exchanged(values, axis, count):
    arrived = {0: values[0]}
    for k in sorted(range(1, count), key=lambda k: abs(k - count / 2)):
        arrived[k] = lax.ppermute(values[k], axis, rotation(count, k))
    return [arrived[k] for k in range(count)]


def per_device(initial, coil_maps, kspace, sampled, first_w, time_w, last_w):
    section_no = lax.axis_index("cascade")
    sections = lax.axis_size("cascade")
    shares = lax.axis_size("coil")
    readout_parts = lax.axis_size("readout")
    phases = kspace.shape[2]
    part = kspace.shape[-1]
    channels = first_w.shape[-1]

    def rows_of(array):
        return array.reshape(array.shape[:-3] + (2 * array.shape[-3], part))

    def padded(block):
        return jnp.pad(block, ((0, -block.shape[0] % 64), (0, 0)))

    initial, coil_maps, kspace = rows_of(initial), rows_of(coil_maps), rows_of(kspace)
    images = {"all": [initial]}
    matrices = None
    joints = []

    def in_order(near, far, axis):
        return jnp.where(
            far_is_up(),
            jnp.concatenate([near, far], axis),
            jnp.concatenate([far, near], axis),
        )

    for section in range(sections):
        parts = {}
        for side, image in images.items():
            partial = consistency(image, coil_maps, kspace, sampled, shares, side)
            if matrices is None:
                partial, (first_w, time_w, last_w) = lax.optimization_barrier(
                    (partial, (first_w, time_w, last_w))
                )
            parts[side] = exchanged(partial, "coil", shares)
        if matrices is None:
            pack = jnp.concatenate(
                [
                    time_w[0].reshape(-1, channels),
                    padded(first_w[0].reshape(-1, channels)),
                    padded(jnp.swapaxes(last_w[0], 1, 2).reshape(-1, channels)),
                ],
                0,
            )
            packs = exchanged([pack] * sections, "cascade", sections)
            matrices = weight_matrices(packs, phases)
            parts, matrices = lax.optimization_barrier((parts, matrices))
        added = {
            side: sum(p.astype(F32) for p in pieces).astype(BF16) for side, pieces in parts.items()
        }
        combined = added["all"] if section == 0 else in_order(added["near"], added["far"], 0)
        even = lax.ppermute(combined, "readout", swaps(readout_parts, 0))
        odd = lax.ppermute(combined, "readout", swaps(readout_parts, 1))
        (sums,) = denoise("alone", combined, matrices, section, phases)
        (sums,) = denoise("near", combined, matrices, section, phases, even, sums)
        if section < sections - 1:
            near, rest = denoise("far", combined, matrices, section, phases, odd, sums)
            far, joint = denoise("last", combined, matrices, section, phases, odd, rest, near)
            images = {
                side: exchanged([value] * shares, "coil", shares)
                for side, value in (("near", near), ("far", far))
            }

        else:
            (joint,) = denoise("end", combined, matrices, section, phases, odd, sums)
        joints.append(joint)

    def of_section(values, wanted):
        value = values[0]
        for section in range(1, sections):
            value = jnp.where(wanted == section, values[section], value)
        return value

    pieces = exchanged(
        [of_section(joints, (section_no + k) % sections) for k in range(sections)],
        "cascade",
        sections,
    )
    arrived = []
    for block in range(sections):
        value = pieces[0]
        for k in range(1, sections):
            value = jnp.where((section_no - block) % sections == k, pieces[k], value)
        arrived.append(value)
    result = jnp.stack(arrived)[None]
    return result.reshape(result.shape[:-2] + (result.shape[-2] // 2, 2, part))


def solution(mesh):
    in_specs = (
        P(None, None, "readout", None, None, None),
        P(None, "coil", "readout", None, None, None),
        P(None, "coil", None, "readout", None, None, None),
        P("coil", None, None, None),
        P("cascade", None, None, None),
        P("cascade", None, None, None),
        P("cascade", None, None, None),
    )
    out_specs = P("cascade", None, None, "readout", "coil", None, None)
    return jax.shard_map(
        per_device, mesh=mesh, in_specs=in_specs, out_specs=out_specs, check_vma=False
    )
```

```python
import functools

import jax
import jax.numpy as jnp
import numpy as np
from jax import lax
from jax.experimental import pallas as pl
from jax.experimental.pallas import tpu as pltpu
from jax.sharding import PartitionSpec as P

F32 = jnp.float32
BF16 = jnp.bfloat16
HALO = 2
BATCH = 16
VMEM_LIMIT = 30 * 1024 * 1024


def fourier_pair(length):
    positions = np.arange(length, dtype=np.int64)
    angles = (positions[:, None] * positions[None, :] % length) * (2.0 * np.pi / length)
    factor = 1.0 / np.sqrt(float(length))
    return np.cos(angles) * factor, np.sin(angles) * factor


def bf16(values):
    return jnp.asarray(values.astype(jnp.bfloat16))


def column_matrix(length, direction):
    cosine, sine = fourier_pair(length)
    return np.block([[cosine, direction * sine], [-direction * sine, cosine]])


def parts_apart(length):
    rows = np.arange(2 * length).reshape(length, 2).T.reshape(-1)
    return np.eye(2 * length)[rows]


@functools.lru_cache(maxsize=None)
def consistency_tables(line_total, part_total, phases, share):
    tables = [
        column_matrix(part_total, -1.0),
        column_matrix(line_total, -1.0).T,
        column_matrix(line_total, 1.0).T,
        column_matrix(part_total, 1.0),
        parts_apart(line_total),
        line_major(phases, share),
    ]
    size = max(max(t.shape) for t in tables)
    stacked = np.zeros((len(tables), size, size))
    for index, table in enumerate(tables):
        stacked[index, : table.shape[0], : table.shape[1]] = table
    return stacked


def line_major(phases, share):
    rows = np.arange(phases * 2 * share).reshape(phases * 2, share).T.reshape(-1)
    return np.eye(phases * 2 * share)[rows]


def phase_inside(phases, share):
    rows = np.arange(phases * share * 2).reshape(phases, share, 2).transpose(1, 0, 2).reshape(-1)
    return np.eye(phases * share * 2)[rows]


def dot(left, right):
    return jnp.dot(left, right, preferred_element_type=F32)


def far_is_up():
    return lax.rem(lax.axis_index("readout"), 2) == 1


def side_count(side, readouts):
    return {"all": readouts, "near": readouts - 1, "far": 1}[side]


def side_rows(side, readouts):
    if side == "all":
        return list(range(readouts))
    up = far_is_up().astype(jnp.int32)
    if side == "far":
        return [up * (readouts - 1)]
    return [1 - up + k for k in range(readouts - 1)]


def consistency_kernel(*refs, pieces, shares, edge, batch, direct, side):
    images, refs = refs[:pieces], refs[pieces:]
    maps, samples, mask, tables = refs[:4]
    outs = refs[4 : 4 + shares]
    window, joined, refs = refs[4 + shares], refs[5 + shares], refs[6 + shares :]
    block, me = lax.axis_index("cascade"), lax.axis_index("coil")
    coils, phases, every, rows, part = samples.shape[1:]
    chosen = side_rows(side, every)
    readouts = len(chosen)
    count = rows // 2
    share = count // shares

    if direct:
        waits = {}
        maps, samples = maps.at[block], samples.at[block]
    else:
        sems = refs[-1]
        sources = (tables, images[0].at[block], maps.at[block], mask, samples.at[block])
        names = ("tables", "image", "maps", "mask", "samples")
        waits = {}
        for k, (name, source) in enumerate(zip(names, sources)):
            waits[name] = pltpu.make_async_copy(source, refs[k], sems.at[k])
        for name in names:
            waits[name].start()
        tables, image, maps, mask, samples = refs[:5]

    def wait(name):
        if name in waits:
            waits.pop(name).wait()

    wait("tables")
    wait("image")
    if pieces > 1:
        image = joined
        for k in range(pieces):
            to = pl.multiple_of(lax.rem(me + (pieces - k), pieces) * 2 * share, 2 * share)
            joined[:, :, pl.ds(to, 2 * share)] = images[k][...]

    def apart(values):
        return dot(tables[4, :rows, :rows], values)

    def lane(n):
        return slice(n * part, (n + 1) * part)

    def band(n):
        return slice(n * count, (n + 1) * count)

    places = [(r, p) for r in range(readouts) for p in range(phases)]
    image_now = apart(jnp.concatenate([image[p, r] for r, p in places], 1))
    wait("maps")
    maps_now = apart(
        jnp.concatenate([maps[coil, r] for r in chosen for coil in range(coils)], 1)
    )

    def map_parts(r, coil):
        where = lane(r * coils + coil)
        return maps_now[:count, where], maps_now[count:, where]

    slabs = [(r, coil, p) for r in range(readouts) for coil in range(coils) for p in range(phases)]
    real_sum = {place: 0.0 for place in places}
    imag_sum = {place: 0.0 for place in places}
    for begin in range(0, len(slabs), batch):
        group = slabs[begin : begin + batch]
        every = range(len(group))
        fields = []
        for r, coil, p in group:
            map_real, map_imag = map_parts(r, coil)
            where = lane(places.index((r, p)))
            real, imag = image_now[:count, where], image_now[count:, where]
            fields.append(
                jnp.concatenate(
                    [
                        (map_real * real - map_imag * imag).astype(BF16),
                        (map_real * imag + map_imag * real).astype(BF16),
                    ],
                    1,
                )
            )
        half = dot(jnp.concatenate(fields, 0), tables[0, : 2 * part, : 2 * part]).astype(BF16)
        stacked = jnp.concatenate(
            [jnp.concatenate([half[band(n), :part], half[band(n), part:]], 0) for n in every], 1
        )
        spectrum = dot(tables[1, :rows, :rows], stacked)
        wait("mask")
        wait("samples")
        measured = apart(
            jnp.concatenate([samples[coil, p, chosen[r]] for r, coil, p in group], 1)
        )
        acquired = jnp.concatenate([mask[coil, p] for r, coil, p in group], 1) != 0
        mixed = jnp.concatenate(
            [
                jnp.where(acquired, measured[:count], spectrum[:count]).astype(BF16),
                jnp.where(acquired, measured[count:], spectrum[count:]).astype(BF16),
            ],
            0,
        )
        back = dot(tables[2, :rows, :rows], mixed).astype(BF16)
        paired = jnp.concatenate(
            [jnp.concatenate([back[:count, lane(n)], back[count:, lane(n)]], 1) for n in every], 0
        )
        restored = dot(paired, tables[3, : 2 * part, : 2 * part])
        for n, (r, coil, p) in enumerate(group):
            map_real, map_imag = map_parts(r, coil)
            real, imag = restored[band(n), :part], restored[band(n), part:]
            real_sum[r, p] = real_sum[r, p] + (map_real * real + map_imag * imag)
            imag_sum[r, p] = imag_sum[r, p] + (map_real * imag - map_imag * real)

    blocks = []
    for r in range(readouts):
        summed = [
            v.astype(BF16) for p in range(phases) for v in (real_sum[r, p], imag_sum[r, p])
        ]
        blocks += [
            jnp.concatenate([v[k * share : (k + 1) * share] for v in summed], 0)
            for k in range(shares)
        ]
    width = phases * 2 * share
    ordered = dot(tables[5, :width, :width], jnp.concatenate(blocks, 1)).astype(BF16)
    border = jnp.zeros((edge, part), BF16)
    for r in range(readouts):
        window[r, 0:edge] = border
        window[r, edge + shares * width : 2 * edge + shares * width] = border
        for k in range(shares):
            window[r, edge + k * width : edge + (k + 1) * width] = ordered[:, lane(r * shares + k)]
    for k in range(shares):
        begin = pl.multiple_of(lax.rem(me + k, shares) * width, width)
        outs[k][...] = window[:, pl.ds(begin, width + 2 * edge)]


def consistency(images, maps, samples, mask, shares, side):
    blocks, coils, phases, every, rows, part = samples.shape
    readouts = side_count(side, every)
    lines = rows // 2
    share_rows = rows // shares
    edge = HALO * phases * 2
    tables = bf16(consistency_tables(lines, part, phases, lines // shares))
    pieces = len(images)
    direct = pieces > 1
    width = phases * share_rows + 2 * edge
    body = functools.partial(
        consistency_kernel, pieces=pieces, shares=shares, edge=edge, batch=BATCH, direct=direct, side=side
    )
    image_shape = (phases, readouts, rows, part)
    buffers = [
        pltpu.VMEM(tables.shape, BF16),
        pltpu.VMEM(image_shape, BF16),
        pltpu.VMEM((coils, every, rows, part), BF16),
        pltpu.VMEM((coils, phases, lines, part), jnp.int32),
        pltpu.VMEM((coils, phases, every, rows, part), BF16),
        pltpu.SemaphoreType.DMA((5,)),
    ]
    return pl.pallas_call(
        body,
        in_specs=[pl.BlockSpec(memory_space=pltpu.VMEM if direct else pl.ANY)] * (pieces + 4),
        out_specs=[pl.BlockSpec(memory_space=pltpu.VMEM)] * shares,
        scratch_shapes=[
            pltpu.VMEM((readouts, shares * phases * share_rows + 2 * edge, part), BF16),
            pltpu.VMEM(image_shape if direct else (16, part), BF16),
        ]
        + ([] if direct else buffers),
        out_shape=[jax.ShapeDtypeStruct((readouts, width, part), BF16)] * shares,
        compiler_params=pltpu.CompilerParams(
            vmem_limit_bytes=VMEM_LIMIT
        ),
        cost_estimate=pl.CostEstimate(
            flops=readouts * coils * phases * rows * part * rows * 20,
            bytes_accessed=4 * 1024 * 1024,
            transcendentals=0,
        ),
        name="consistency",
    )(*[x if direct else pltpu.with_memory_space_constraint(x, pltpu.HBM) for x in (*images, maps, samples, mask, tables)])


def tap_rows(phases, parts):
    rows = []
    for row_shift in range(3):
        for tap in range(9):
            for phase in range(phases):
                for piece in range(parts):
                    rows.append(((9 * row_shift + tap) * parts + piece, phase))
        rows += [(-1, -1)] * (-(9 * phases * parts) % 16)
    return rows


@functools.lru_cache(maxsize=None)
def weight_tables(phases, channels):
    rows = tap_rows(phases, 2)
    spread = np.zeros((len(rows), 64))
    own_phase = np.zeros((len(rows), phases * channels))
    for index, (source, phase) in enumerate(rows):
        if source >= 0:
            spread[index, source] = 1.0
            own_phase[index, phase * channels : (phase + 1) * channels] = 1.0
    tiled = np.tile(np.eye(channels), (1, phases))
    phase_of = np.repeat(np.arange(phases), channels)
    time_masks = np.stack(
        [phase_of[None, :] - phase_of[:, None] == 2 * (k - 1) for k in range(3)]
    ).astype(np.float64)
    return spread, own_phase, tiled, time_masks


def weights_kernel(*refs, pieces):
    packs = refs[:pieces]
    spread, spread_t, own_phase, own_phase_t, tiled, tiled_t, time_masks = refs[pieces : pieces + 7]
    first_out, time_out, last_out = refs[pieces + 7 :]
    channels = tiled.shape[0]
    me = lax.axis_index("cascade")

    def transposed(block):
        return lax.dot_general(
            tiled_t[...], block, (((1,), (1,)), ((), ())), preferred_element_type=F32
        ).astype(BF16)

    for section in range(pieces):
        pick = lax.rem(me - section + pieces, pieces)
        pack = packs[0][...].astype(F32)
        for k in range(1, pieces):
            pack = jnp.where(pick == k, packs[k][...].astype(F32), pack)
        pack = pack.astype(BF16)
        time = 0.0
        for k in range(3):
            block = transposed(pack[k * channels : (k + 1) * channels])
            time = time + dot(block, tiled[...]) * time_masks[k].astype(F32)
        time_out[section] = time.astype(BF16)
        first = transposed(pack[3 * channels : 3 * channels + 64])
        first_out[section] = (dot(first, spread_t[...]) * own_phase_t[...].astype(F32)).astype(BF16)
        last = dot(spread[...], pack[3 * channels + 64 :]).astype(BF16)
        last_out[section] = (dot(last, tiled[...]) * own_phase[...].astype(F32)).astype(BF16)


def weight_matrices(packs, phases):
    sections = len(packs)
    channels = packs[0].shape[1]
    spread, own_phase, tiled, time_masks = weight_tables(phases, channels)
    tables = [
        bf16(t) for t in (spread, spread.T, own_phase, own_phase.T, tiled, tiled.T, time_masks)
    ]
    wide = phases * channels
    taps = spread.shape[0]
    shapes = [(wide, taps), (wide, wide), (taps, wide)]
    return pl.pallas_call(
        functools.partial(weights_kernel, pieces=sections),
        in_specs=[pl.BlockSpec(memory_space=pltpu.VMEM)] * (sections + len(tables)),
        out_specs=[pl.BlockSpec(memory_space=pltpu.VMEM)] * len(shapes),
        out_shape=[jax.ShapeDtypeStruct((sections,) + s, BF16) for s in shapes],
        compiler_params=pltpu.CompilerParams(vmem_limit_bytes=VMEM_LIMIT),
        cost_estimate=pl.CostEstimate(
            flops=sections * wide * wide * 1000, bytes_accessed=2 * 1024 * 1024, transcendentals=0
        ),
        name="weights",
    )(*packs, *tables)


def shifted(values, step):
    part = values.shape[1]
    lane = lax.broadcasted_iota(jnp.int32, values.shape, 1)
    if step > 0:
        return jnp.where(lane == 0, 0.0, pltpu.roll(values, 1, 1))
    return jnp.where(lane == part - 1, 0.0, pltpu.roll(values, part - 1, 1))


def denoise_kernel(*refs, phases, section, stage):
    refs = list(refs)
    own = refs.pop(0)
    beside = None if stage == "alone" else refs.pop(0)
    first, time, last = refs[:3]
    refs = refs[3:]
    before = None if stage == "alone" else refs.pop(0)
    if stage == "far":
        apart, out, rest, taps, sums = refs
    elif stage == "last":
        apart, done, out, joint, taps, sums = refs
    elif stage == "end":
        apart, out, taps, sums = refs
    else:
        sums, taps = refs
    readouts, span, part = own.shape
    cell = 2 * phases
    lines = span // cell
    group = taps.shape[2]
    used = 9 * cell
    readout_no, coil_no = lax.axis_index("readout"), lax.axis_index("coil")
    upward = jnp.logical_not(far_is_up()) if stage == "near" else far_is_up()
    there = jnp.where(upward, readout_no < lax.axis_size("readout") - 1, readout_no > 0)
    first_line = (coil_no > 0).astype(F32).astype(BF16)
    last_line = (coil_no < lax.axis_size("coil") - 1).astype(F32).astype(BF16)

    def neighbour(k):
        if beside is None:
            return jnp.zeros((span, part), F32)
        low = beside[readouts - 1 - k].astype(F32)
        return jnp.where(there, jnp.where(upward, beside[k].astype(F32), low), 0.0)

    def inwards(k):
        return jnp.where(upward, own[readouts - 1 - k].astype(F32), own[k].astype(F32))

    def fill_taps(slabs):
        filler = [jnp.zeros((group - used, part), F32)] if group > used else []
        for k, slab in enumerate(slabs):
            index = jnp.where(upward, k, len(slabs) - 1 - k)
            views = [shifted(slab, 1), slab, shifted(slab, -1)]
            for line in range(1, lines - 1):
                around = [
                    views[e][cell * (line + c - 1) : cell * (line + c)]
                    for c in range(3)
                    for e in range(3)
                ]
                taps[index, line - 1] = jnp.concatenate(around + filler, 0).astype(BF16)

    def add_row(start, begun, count, target):
        block = range(1, lines - 1)
        near = jnp.concatenate(
            [taps[pl.ds(start, 3), line - 1].reshape(3 * group, part) for line in block], 1
        )
        hidden = jnp.maximum(dot(first[section], near), 0.0).astype(BF16)
        mixed = jnp.maximum(hidden.astype(F32) + dot(time[section], hidden), 0.0).astype(BF16)
        edge = (len(block) - 1) * part
        mixed = jnp.concatenate(
            [mixed[:, :part] * first_line, mixed[:, part:edge], mixed[:, edge:] * last_line], 1
        )
        chosen = pl.ds(pl.multiple_of(begun * group, 16), count * group)
        result = dot(last[section, chosen], mixed)
        for a in range(count):
            for e in range(3):
                for line in range(lines):
                    terms = []
                    for c in range(3):
                        source = line + c - 2
                        if 0 <= source < len(block):
                            at = a * group + (3 * c + e) * cell
                            terms.append(
                                result[at : at + cell, source * part : (source + 1) * part]
                            )
                    sums[e, target - a, line * cell : (line + 1) * cell] += sum(
                        terms[1:], terms[0]
                    )

    def add_outer(start, target):
        add_row(start, jnp.where(upward, 2, 0), 1, target)

    def add_inner(start):
        add_row(start, jnp.where(upward, 1, 0), 2, jnp.where(upward, readouts - 1, 1))

    def finished(rows):
        body = slice(HALO * cell, span - HALO * cell)
        finals = []
        for r, at in rows:
            left, here, right = [sums[e, at, body] for e in range(3)]
            value = own[r, body].astype(F32) + here + shifted(left, 1) + shifted(right, -1)
            finals.append(value.astype(BF16))
        ordered = dot(apart[...], jnp.concatenate(finals, 1)).astype(BF16)
        height = out.shape[2]
        for p in range(phases):
            for k in range(len(rows)):
                out[p, k] = ordered[p * height : (p + 1) * height, k * part : (k + 1) * part]

    sums[...] = jnp.zeros_like(sums) if before is None else before[...]
    if stage == "near":
        fill_taps([inwards(k) for k in reversed(range(readouts))] + [neighbour(0), neighbour(1)])
        pl.when(there)(lambda: add_outer(jnp.where(upward, readouts - 1, 0), jnp.where(upward, readouts - 1, 0)))
        add_inner(jnp.where(upward, readouts - 2, 1))
        for row in range(1, readouts - 1):
            add_row(row - 1 + jnp.where(upward, 0, HALO), 0, 3, row + 1)
    elif stage == "end":

        @pl.when(there)
        def _():
            fill_taps([inwards(1), inwards(0), neighbour(0), neighbour(1)])
            add_outer(jnp.where(upward, 1, 0), jnp.where(upward, readouts - 1, 0))
            add_inner(jnp.where(upward, 0, 1))

        finished([(row, row) for row in range(readouts)])
    elif stage == "last":

        @pl.when(there)
        def _():
            fill_taps([inwards(0), neighbour(0), neighbour(1)])
            add_outer(0, 0)

        (row,) = side_rows("far", readouts)
        finished([(row, 0)])
        joint[:, row] = out[:, 0]
        for k, near_row in enumerate(side_rows("near", readouts)):
            joint[:, near_row] = done[:, k]
    else:

        @pl.when(there if stage == "far" else jnp.logical_not(there))
        def _():
            fill_taps([inwards(1), inwards(0), neighbour(0)])
            add_inner(0)

        if stage == "far":
            finished([(row, row) for row in side_rows("near", readouts)])
            (row,) = side_rows("far", readouts)
            rest[:, 0] = sums[:, row]


def denoise(stage, own, matrices, section, phases, beside=None, before=None, done=None):
    readouts, span, part = own.shape
    cell = 2 * phases
    lines = span // cell
    share = lines - 2 * HALO
    group = matrices[0].shape[2] // 3
    operands = [own] + [beside] * (stage != "alone") + list(matrices) + [before] * (stage != "alone")
    sums_shape = (3, 1 if stage == "last" else readouts, span, part)
    depth = {"near": readouts + HALO, "end": 4}.get(stage, 3)
    scratch = [pltpu.VMEM((depth, lines - 2, group, part), BF16)]

    def image(count):
        return jax.ShapeDtypeStruct((phases, count, 2 * share, part), BF16)

    if stage in ("far", "last", "end"):
        operands.append(bf16(phase_inside(phases, share).T))
        scratch.append(pltpu.VMEM(sums_shape, F32))
    if stage == "far":
        result = [image(readouts - 1), jax.ShapeDtypeStruct((3, 1, span, part), F32)]
    elif stage == "last":
        operands.append(done)
        result = [image(1), image(readouts)]
    elif stage == "end":
        result = [image(readouts)]
    else:
        result = [jax.ShapeDtypeStruct(sums_shape, F32)]
    return pl.pallas_call(
        functools.partial(denoise_kernel, phases=phases, section=section, stage=stage),
        in_specs=[pl.BlockSpec(memory_space=pltpu.VMEM)] * len(operands),
        out_specs=[pl.BlockSpec(memory_space=pltpu.VMEM)] * len(result),
        scratch_shapes=scratch,
        out_shape=result,
        compiler_params=pltpu.CompilerParams(vmem_limit_bytes=VMEM_LIMIT),
        cost_estimate=pl.CostEstimate(
            flops={"alone": 1, "near": 6, "far": 3, "last": 3, "end": 6}[stage]
            * (readouts * lines * part * 256 * 256),
            bytes_accessed=2 * 1024 * 1024,
            transcendentals=0,
        ),
        name="denoise_" + stage,
    )(*operands)


def rotation(count, step):
    return [(i, (i + step) % count) for i in range(count)]


def swaps(count, first):
    pairs = [(i, (i + 1) % count) for i in range(first, count, 2)]
    return pairs + [(target, source) for source, target in pairs]


def exchanged(values, axis, count):
    arrived = {0: values[0]}
    for k in sorted(range(1, count), key=lambda k: abs(k - count / 2)):
        arrived[k] = lax.ppermute(values[k], axis, rotation(count, k))
    return [arrived[k] for k in range(count)]


def per_device(initial, coil_maps, kspace, sampled, first_w, time_w, last_w):
    section_no = lax.axis_index("cascade")
    sections = lax.axis_size("cascade")
    shares = lax.axis_size("coil")
    readout_parts = lax.axis_size("readout")
    phases = kspace.shape[2]
    part = kspace.shape[-1]
    channels = first_w.shape[-1]

    def rows_of(array):
        return array.reshape(array.shape[:-3] + (2 * array.shape[-3], part))

    def padded(block):
        return jnp.pad(block, ((0, -block.shape[0] % 64), (0, 0)))

    initial, coil_maps, kspace = rows_of(initial), rows_of(coil_maps), rows_of(kspace)
    images = {"all": [initial]}
    matrices = None
    joints = []

    def in_order(near, far, axis):
        return jnp.where(
            far_is_up(),
            jnp.concatenate([near, far], axis),
            jnp.concatenate([far, near], axis),
        )

    for section in range(sections):
        parts = {}
        for side, image in images.items():
            partial = consistency(image, coil_maps, kspace, sampled, shares, side)
            if matrices is None:
                partial, (first_w, time_w, last_w) = lax.optimization_barrier(
                    (partial, (first_w, time_w, last_w))
                )
            parts[side] = exchanged(partial, "coil", shares)
        if matrices is None:
            pack = jnp.concatenate(
                [
                    time_w[0].reshape(-1, channels),
                    padded(first_w[0].reshape(-1, channels)),
                    padded(jnp.swapaxes(last_w[0], 1, 2).reshape(-1, channels)),
                ],
                0,
            )
            packs = exchanged([pack] * sections, "cascade", sections)
            matrices = weight_matrices(packs, phases)
            parts, matrices = lax.optimization_barrier((parts, matrices))
        added = {
            side: sum(p.astype(F32) for p in pieces).astype(BF16) for side, pieces in parts.items()
        }
        combined = added["all"] if section == 0 else in_order(added["near"], added["far"], 0)
        even = lax.ppermute(combined, "readout", swaps(readout_parts, 0))
        odd = lax.ppermute(combined, "readout", swaps(readout_parts, 1))
        (sums,) = denoise("alone", combined, matrices, section, phases)
        (sums,) = denoise("near", combined, matrices, section, phases, even, sums)
        if section < sections - 1:
            near, rest = denoise("far", combined, matrices, section, phases, odd, sums)
            far, joint = denoise("last", combined, matrices, section, phases, odd, rest, near)
            images = {
                side: exchanged([value] * shares, "coil", shares)
                for side, value in (("near", near), ("far", far))
            }

        else:
            (joint,) = denoise("end", combined, matrices, section, phases, odd, sums)
        joints.append(joint)

    def of_section(values, wanted):
        value = values[0]
        for section in range(1, sections):
            value = jnp.where(wanted == section, values[section], value)
        return value

    pieces = exchanged(
        [of_section(joints, (section_no + k) % sections) for k in range(sections)],
        "cascade",
        sections,
    )
    result = jnp.zeros((sections,) + joints[0].shape, BF16)
    for k in range(sections):
        place = lax.rem(section_no - k + sections, sections)
        result = lax.dynamic_update_slice_in_dim(result, pieces[k][None], place, 0)
    result = result[None]
    return result.reshape(result.shape[:-2] + (result.shape[-2] // 2, 2, part))


def solution(mesh):
    in_specs = (
        P(None, None, "readout", None, None, None),
        P(None, "coil", "readout", None, None, None),
        P(None, "coil", None, "readout", None, None, None),
        P("coil", None, None, None),
        P("cascade", None, None, None),
        P("cascade", None, None, None),
        P("cascade", None, None, None),
    )
    out_specs = P("cascade", None, None, "readout", "coil", None, None)
    return jax.shard_map(
        per_device, mesh=mesh, in_specs=in_specs, out_specs=out_specs, check_vma=False
    )
```

```python
import functools

import jax
import jax.numpy as jnp
import numpy as np
from jax import lax
from jax.experimental import pallas as pl
from jax.experimental.pallas import tpu as pltpu
from jax.sharding import PartitionSpec as P

F32 = jnp.float32
BF16 = jnp.bfloat16
HALO = 2
BATCH = 16
VMEM_LIMIT = 30 * 1024 * 1024


def fourier_pair(length):
    positions = np.arange(length, dtype=np.int64)
    angles = (positions[:, None] * positions[None, :] % length) * (2.0 * np.pi / length)
    factor = 1.0 / np.sqrt(float(length))
    return np.cos(angles) * factor, np.sin(angles) * factor


def bf16(values):
    return jnp.asarray(values.astype(jnp.bfloat16))


def column_matrix(length, direction):
    cosine, sine = fourier_pair(length)
    return np.block([[cosine, direction * sine], [-direction * sine, cosine]])


def parts_apart(length):
    rows = np.arange(2 * length).reshape(length, 2).T.reshape(-1)
    return np.eye(2 * length)[rows]


@functools.lru_cache(maxsize=None)
def consistency_tables(line_total, part_total, phases, share):
    tables = [
        column_matrix(part_total, -1.0),
        column_matrix(line_total, -1.0).T,
        column_matrix(line_total, 1.0).T,
        column_matrix(part_total, 1.0),
        parts_apart(line_total),
        line_major(phases, share),
    ]
    size = max(max(t.shape) for t in tables)
    kept, places = [], []
    for table in tables:
        padded = np.zeros((size, size))
        padded[: table.shape[0], : table.shape[1]] = table
        same = [k for k, other in enumerate(kept) if np.array_equal(other, padded)]
        places.append(same[0] if same else len(kept))
        if not same:
            kept.append(padded)
    return np.stack(kept), tuple(places)


def line_major(phases, share):
    rows = np.arange(phases * 2 * share).reshape(phases * 2, share).T.reshape(-1)
    return np.eye(phases * 2 * share)[rows]


def phase_inside(phases, share):
    rows = np.arange(phases * share * 2).reshape(phases, share, 2).transpose(1, 0, 2).reshape(-1)
    return np.eye(phases * share * 2)[rows]


def dot(left, right):
    return jnp.dot(left, right, preferred_element_type=F32)


def far_is_up():
    return lax.rem(lax.axis_index("readout"), 2) == 1


def side_count(side, readouts):
    return {"all": readouts, "near": readouts - 1, "far": 1}[side]


def side_rows(side, readouts):
    if side == "all":
        return list(range(readouts))
    up = far_is_up().astype(jnp.int32)
    if side == "far":
        return [up * (readouts - 1)]
    return [1 - up + k for k in range(readouts - 1)]


def consistency_kernel(*refs, pieces, shares, edge, batch, direct, side, table_at):
    images, refs = refs[:pieces], refs[pieces:]
    maps, samples, mask, tables = refs[:4]
    outs = refs[4 : 4 + shares]
    window, joined, refs = refs[4 + shares], refs[5 + shares], refs[6 + shares :]
    block, me = lax.axis_index("cascade"), lax.axis_index("coil")
    coils, phases, every, rows, part = samples.shape[1:]
    chosen = side_rows(side, every)
    readouts = len(chosen)
    count = rows // 2
    share = count // shares

    if direct:
        waits = {}
        maps, samples = maps.at[block], samples.at[block]
    else:
        sems = refs[-1]
        sources = (tables, images[0].at[block], maps.at[block], mask, samples.at[block])
        names = ("tables", "image", "maps", "mask", "samples")
        waits = {}
        for k, (name, source) in enumerate(zip(names, sources)):
            waits[name] = pltpu.make_async_copy(source, refs[k], sems.at[k])
        for name in names:
            waits[name].start()
        tables, image, maps, mask, samples = refs[:5]

    def wait(name):
        if name in waits:
            waits.pop(name).wait()

    wait("tables")
    wait("image")
    if pieces > 1:
        image = joined
        for k in range(pieces):
            to = pl.multiple_of(lax.rem(me + (pieces - k), pieces) * 2 * share, 2 * share)
            joined[:, :, pl.ds(to, 2 * share)] = images[k][...]

    def apart(values):
        return dot(tables[table_at[4], :rows, :rows], values)

    def lane(n):
        return slice(n * part, (n + 1) * part)

    def band(n):
        return slice(n * count, (n + 1) * count)

    places = [(r, p) for r in range(readouts) for p in range(phases)]
    image_now = apart(jnp.concatenate([image[p, r] for r, p in places], 1))
    wait("maps")
    maps_now = apart(
        jnp.concatenate([maps[coil, r] for r in chosen for coil in range(coils)], 1)
    )

    def map_parts(r, coil):
        where = lane(r * coils + coil)
        return maps_now[:count, where], maps_now[count:, where]

    slabs = [(r, coil, p) for r in range(readouts) for coil in range(coils) for p in range(phases)]
    real_sum = {place: 0.0 for place in places}
    imag_sum = {place: 0.0 for place in places}
    for begin in range(0, len(slabs), batch):
        group = slabs[begin : begin + batch]
        every = range(len(group))
        fields = []
        for r, coil, p in group:
            map_real, map_imag = map_parts(r, coil)
            where = lane(places.index((r, p)))
            real, imag = image_now[:count, where], image_now[count:, where]
            fields.append(
                jnp.concatenate(
                    [
                        (map_real * real - map_imag * imag).astype(BF16),
                        (map_real * imag + map_imag * real).astype(BF16),
                    ],
                    1,
                )
            )
        half = dot(jnp.concatenate(fields, 0), tables[table_at[0], : 2 * part, : 2 * part]).astype(BF16)
        stacked = jnp.concatenate(
            [jnp.concatenate([half[band(n), :part], half[band(n), part:]], 0) for n in every], 1
        )
        spectrum = dot(tables[table_at[1], :rows, :rows], stacked)
        wait("mask")
        wait("samples")
        measured = apart(
            jnp.concatenate([samples[coil, p, chosen[r]] for r, coil, p in group], 1)
        )
        acquired = jnp.concatenate([mask[coil, p] for r, coil, p in group], 1) != 0
        mixed = jnp.concatenate(
            [
                jnp.where(acquired, measured[:count], spectrum[:count]).astype(BF16),
                jnp.where(acquired, measured[count:], spectrum[count:]).astype(BF16),
            ],
            0,
        )
        back = dot(tables[table_at[2], :rows, :rows], mixed).astype(BF16)
        paired = jnp.concatenate(
            [jnp.concatenate([back[:count, lane(n)], back[count:, lane(n)]], 1) for n in every], 0
        )
        restored = dot(paired, tables[table_at[3], : 2 * part, : 2 * part])
        for n, (r, coil, p) in enumerate(group):
            map_real, map_imag = map_parts(r, coil)
            real, imag = restored[band(n), :part], restored[band(n), part:]
            real_sum[r, p] = real_sum[r, p] + (map_real * real + map_imag * imag)
            imag_sum[r, p] = imag_sum[r, p] + (map_real * imag - map_imag * real)

    blocks = []
    for r in range(readouts):
        summed = [
            v.astype(BF16) for p in range(phases) for v in (real_sum[r, p], imag_sum[r, p])
        ]
        blocks += [
            jnp.concatenate([v[k * share : (k + 1) * share] for v in summed], 0)
            for k in range(shares)
        ]
    width = phases * 2 * share
    ordered = dot(tables[table_at[5], :width, :width], jnp.concatenate(blocks, 1)).astype(BF16)
    border = jnp.zeros((edge, part), BF16)
    for r in range(readouts):
        window[r, 0:edge] = border
        window[r, edge + shares * width : 2 * edge + shares * width] = border
        for k in range(shares):
            window[r, edge + k * width : edge + (k + 1) * width] = ordered[:, lane(r * shares + k)]
    for k in range(shares):
        begin = pl.multiple_of(lax.rem(me + k, shares) * width, width)
        outs[k][...] = window[:, pl.ds(begin, width + 2 * edge)]


def consistency(images, maps, samples, mask, shares, side):
    blocks, coils, phases, every, rows, part = samples.shape
    readouts = side_count(side, every)
    lines = rows // 2
    share_rows = rows // shares
    edge = HALO * phases * 2
    tables, places = consistency_tables(lines, part, phases, lines // shares)
    tables = bf16(tables)
    pieces = len(images)
    direct = pieces > 1
    width = phases * share_rows + 2 * edge
    body = functools.partial(
        consistency_kernel, pieces=pieces, shares=shares, edge=edge, batch=BATCH, direct=direct, side=side,
        table_at=places
    )
    image_shape = (phases, readouts, rows, part)
    buffers = [
        pltpu.VMEM(tables.shape, BF16),
        pltpu.VMEM(image_shape, BF16),
        pltpu.VMEM((coils, every, rows, part), BF16),
        pltpu.VMEM((coils, phases, lines, part), jnp.int32),
        pltpu.VMEM((coils, phases, every, rows, part), BF16),
        pltpu.SemaphoreType.DMA((5,)),
    ]
    return pl.pallas_call(
        body,
        in_specs=[pl.BlockSpec(memory_space=pltpu.VMEM if direct else pl.ANY)] * (pieces + 4),
        out_specs=[pl.BlockSpec(memory_space=pltpu.VMEM)] * shares,
        scratch_shapes=[
            pltpu.VMEM((readouts, shares * phases * share_rows + 2 * edge, part), BF16),
            pltpu.VMEM(image_shape if direct else (16, part), BF16),
        ]
        + ([] if direct else buffers),
        out_shape=[jax.ShapeDtypeStruct((readouts, width, part), BF16)] * shares,
        compiler_params=pltpu.CompilerParams(
            vmem_limit_bytes=VMEM_LIMIT
        ),
        cost_estimate=pl.CostEstimate(
            flops=readouts * coils * phases * rows * part * rows * 20,
            bytes_accessed=4 * 1024 * 1024,
            transcendentals=0,
        ),
        name="consistency",
    )(*[x if direct else pltpu.with_memory_space_constraint(x, pltpu.HBM) for x in (*images, maps, samples, mask, tables)])


def tap_rows(phases, parts):
    rows = []
    for row_shift in range(3):
        for tap in range(9):
            for phase in range(phases):
                for piece in range(parts):
                    rows.append(((9 * row_shift + tap) * parts + piece, phase))
        rows += [(-1, -1)] * (-(9 * phases * parts) % 16)
    return rows


@functools.lru_cache(maxsize=None)
def weight_tables(phases, channels):
    rows = tap_rows(phases, 2)
    spread = np.zeros((len(rows), 64))
    own_phase = np.zeros((len(rows), phases * channels))
    for index, (source, phase) in enumerate(rows):
        if source >= 0:
            spread[index, source] = 1.0
            own_phase[index, phase * channels : (phase + 1) * channels] = 1.0
    tiled = np.tile(np.eye(channels), (1, phases))
    phase_of = np.repeat(np.arange(phases), channels)
    time_masks = np.stack(
        [phase_of[None, :] - phase_of[:, None] == 2 * (k - 1) for k in range(3)]
    ).astype(np.float64)
    return spread, own_phase, tiled, time_masks


def weights_kernel(*refs, pieces):
    packs = refs[:pieces]
    spread, spread_t, own_phase, own_phase_t, tiled, tiled_t, time_masks = refs[pieces : pieces + 7]
    first_out, time_out, last_out = refs[pieces + 7 :]
    channels = tiled.shape[0]
    me = lax.axis_index("cascade")

    def transposed(block):
        return lax.dot_general(
            tiled_t[...], block, (((1,), (1,)), ((), ())), preferred_element_type=F32
        ).astype(BF16)

    for section in range(pieces):
        pick = lax.rem(me - section + pieces, pieces)
        pack = packs[0][...].astype(F32)
        for k in range(1, pieces):
            pack = jnp.where(pick == k, packs[k][...].astype(F32), pack)
        pack = pack.astype(BF16)
        time = 0.0
        for k in range(3):
            block = transposed(pack[k * channels : (k + 1) * channels])
            time = time + dot(block, tiled[...]) * time_masks[k].astype(F32)
        time_out[section] = time.astype(BF16)
        first = transposed(pack[3 * channels : 3 * channels + 64])
        first_out[section] = (dot(first, spread_t[...]) * own_phase_t[...].astype(F32)).astype(BF16)
        last = dot(spread[...], pack[3 * channels + 64 :]).astype(BF16)
        last_out[section] = (dot(last, tiled[...]) * own_phase[...].astype(F32)).astype(BF16)


def weight_matrices(packs, phases):
    sections = len(packs)
    channels = packs[0].shape[1]
    spread, own_phase, tiled, time_masks = weight_tables(phases, channels)
    tables = [
        bf16(t) for t in (spread, spread.T, own_phase, own_phase.T, tiled, tiled.T, time_masks)
    ]
    wide = phases * channels
    taps = spread.shape[0]
    shapes = [(wide, taps), (wide, wide), (taps, wide)]
    return pl.pallas_call(
        functools.partial(weights_kernel, pieces=sections),
        in_specs=[pl.BlockSpec(memory_space=pltpu.VMEM)] * (sections + len(tables)),
        out_specs=[pl.BlockSpec(memory_space=pltpu.VMEM)] * len(shapes),
        out_shape=[jax.ShapeDtypeStruct((sections,) + s, BF16) for s in shapes],
        compiler_params=pltpu.CompilerParams(vmem_limit_bytes=VMEM_LIMIT),
        cost_estimate=pl.CostEstimate(
            flops=sections * wide * wide * 1000, bytes_accessed=2 * 1024 * 1024, transcendentals=0
        ),
        name="weights",
    )(*packs, *tables)


def shifted(values, step):
    part = values.shape[1]
    lane = lax.broadcasted_iota(jnp.int32, values.shape, 1)
    if step > 0:
        return jnp.where(lane == 0, 0.0, pltpu.roll(values, 1, 1))
    return jnp.where(lane == part - 1, 0.0, pltpu.roll(values, part - 1, 1))


def denoise_kernel(*refs, phases, section, stage):
    refs = list(refs)
    own = refs.pop(0)
    beside = None if stage == "alone" else refs.pop(0)
    first, time, last = refs[:3]
    refs = refs[3:]
    before = None if stage == "alone" else refs.pop(0)
    if stage == "far":
        apart, out, rest, taps, sums = refs
    elif stage == "last":
        apart, done, out, joint, taps, sums = refs
    elif stage == "end":
        apart, out, taps, sums = refs
    else:
        sums, taps = refs
    readouts, span, part = own.shape
    cell = 2 * phases
    lines = span // cell
    group = taps.shape[2]
    used = 9 * cell
    readout_no, coil_no = lax.axis_index("readout"), lax.axis_index("coil")
    upward = jnp.logical_not(far_is_up()) if stage == "near" else far_is_up()
    there = jnp.where(upward, readout_no < lax.axis_size("readout") - 1, readout_no > 0)
    first_line = (coil_no > 0).astype(F32).astype(BF16)
    last_line = (coil_no < lax.axis_size("coil") - 1).astype(F32).astype(BF16)

    def neighbour(k):
        if beside is None:
            return jnp.zeros((span, part), F32)
        low = beside[readouts - 1 - k].astype(F32)
        return jnp.where(there, jnp.where(upward, beside[k].astype(F32), low), 0.0)

    def inwards(k):
        return jnp.where(upward, own[readouts - 1 - k].astype(F32), own[k].astype(F32))

    def fill_taps(slabs):
        filler = [jnp.zeros((group - used, part), F32)] if group > used else []
        for k, slab in enumerate(slabs):
            index = jnp.where(upward, k, len(slabs) - 1 - k)
            views = [shifted(slab, 1), slab, shifted(slab, -1)]
            for line in range(1, lines - 1):
                around = [
                    views[e][cell * (line + c - 1) : cell * (line + c)]
                    for c in range(3)
                    for e in range(3)
                ]
                taps[index, line - 1] = jnp.concatenate(around + filler, 0).astype(BF16)

    def add_row(start, begun, count, target):
        block = range(1, lines - 1)
        near = jnp.concatenate(
            [taps[pl.ds(start, 3), line - 1].reshape(3 * group, part) for line in block], 1
        )
        hidden = jnp.maximum(dot(first[section], near), 0.0).astype(BF16)
        mixed = jnp.maximum(hidden.astype(F32) + dot(time[section], hidden), 0.0).astype(BF16)
        edge = (len(block) - 1) * part
        mixed = jnp.concatenate(
            [mixed[:, :part] * first_line, mixed[:, part:edge], mixed[:, edge:] * last_line], 1
        )
        chosen = pl.ds(pl.multiple_of(begun * group, 16), count * group)
        result = dot(last[section, chosen], mixed)
        for a in range(count):
            for e in range(3):
                for line in range(lines):
                    terms = []
                    for c in range(3):
                        source = line + c - 2
                        if 0 <= source < len(block):
                            at = a * group + (3 * c + e) * cell
                            terms.append(
                                result[at : at + cell, source * part : (source + 1) * part]
                            )
                    sums[e, target - a, line * cell : (line + 1) * cell] += sum(
                        terms[1:], terms[0]
                    )

    def add_outer(start, target):
        add_row(start, jnp.where(upward, 2, 0), 1, target)

    def add_inner(start):
        add_row(start, jnp.where(upward, 1, 0), 2, jnp.where(upward, readouts - 1, 1))

    def finished(rows):
        body = slice(HALO * cell, span - HALO * cell)
        finals = []
        for r, at in rows:
            left, here, right = [sums[e, at, body] for e in range(3)]
            value = own[r, body].astype(F32) + here + shifted(left, 1) + shifted(right, -1)
            finals.append(value.astype(BF16))
        ordered = dot(apart[...], jnp.concatenate(finals, 1)).astype(BF16)
        height = out.shape[2]
        for p in range(phases):
            for k in range(len(rows)):
                out[p, k] = ordered[p * height : (p + 1) * height, k * part : (k + 1) * part]

    if stage == "near":
        alone = jnp.where(
            far_is_up(), readout_no == lax.axis_size("readout") - 1, readout_no == 0
        )

        @pl.when(alone)
        def _():
            sums[...] = before[...]

        @pl.when(jnp.logical_not(alone))
        def _():
            sums[...] = jnp.zeros_like(sums)

    elif stage != "alone":
        sums[...] = before[...]
    if stage == "near":
        fill_taps([inwards(k) for k in reversed(range(readouts))] + [neighbour(0), neighbour(1)])
        pl.when(there)(lambda: add_outer(jnp.where(upward, readouts - 1, 0), jnp.where(upward, readouts - 1, 0)))
        add_inner(jnp.where(upward, readouts - 2, 1))
        for row in range(1, readouts - 1):
            add_row(row - 1 + jnp.where(upward, 0, HALO), 0, 3, row + 1)
    elif stage == "end":

        @pl.when(there)
        def _():
            fill_taps([inwards(1), inwards(0), neighbour(0), neighbour(1)])
            add_outer(jnp.where(upward, 1, 0), jnp.where(upward, readouts - 1, 0))
            add_inner(jnp.where(upward, 0, 1))

        finished([(row, row) for row in range(readouts)])
    elif stage == "last":

        @pl.when(there)
        def _():
            fill_taps([inwards(0), neighbour(0), neighbour(1)])
            add_outer(0, 0)

        (row,) = side_rows("far", readouts)
        finished([(row, 0)])
        joint[:, row] = out[:, 0]
        for k, near_row in enumerate(side_rows("near", readouts)):
            joint[:, near_row] = done[:, k]
    else:

        @pl.when(there if stage == "far" else jnp.logical_not(there))
        def _():
            if stage == "alone":
                sums[...] = jnp.zeros_like(sums)
            fill_taps([inwards(1), inwards(0), neighbour(0)])
            add_inner(0)

        if stage == "far":
            finished([(row, row) for row in side_rows("near", readouts)])
            (row,) = side_rows("far", readouts)
            rest[:, 0] = sums[:, row]


def denoise(stage, own, matrices, section, phases, beside=None, before=None, done=None):
    readouts, span, part = own.shape
    cell = 2 * phases
    lines = span // cell
    share = lines - 2 * HALO
    group = matrices[0].shape[2] // 3
    operands = [own] + [beside] * (stage != "alone") + list(matrices) + [before] * (stage != "alone")
    sums_shape = (3, 1 if stage == "last" else readouts, span, part)
    depth = {"near": readouts + HALO, "end": 4}.get(stage, 3)
    scratch = [pltpu.VMEM((depth, lines - 2, group, part), BF16)]

    def image(count):
        return jax.ShapeDtypeStruct((phases, count, 2 * share, part), BF16)

    if stage in ("far", "last", "end"):
        operands.append(bf16(phase_inside(phases, share).T))
        scratch.append(pltpu.VMEM(sums_shape, F32))
    if stage == "far":
        result = [image(readouts - 1), jax.ShapeDtypeStruct((3, 1, span, part), F32)]
    elif stage == "last":
        operands.append(done)
        result = [image(1), image(readouts)]
    elif stage == "end":
        result = [image(readouts)]
    else:
        result = [jax.ShapeDtypeStruct(sums_shape, F32)]
    return pl.pallas_call(
        functools.partial(denoise_kernel, phases=phases, section=section, stage=stage),
        in_specs=[pl.BlockSpec(memory_space=pltpu.VMEM)] * len(operands),
        out_specs=[pl.BlockSpec(memory_space=pltpu.VMEM)] * len(result),
        scratch_shapes=scratch,
        out_shape=result,
        compiler_params=pltpu.CompilerParams(vmem_limit_bytes=VMEM_LIMIT),
        cost_estimate=pl.CostEstimate(
            flops={"alone": 1, "near": 6, "far": 3, "last": 3, "end": 6}[stage]
            * (readouts * lines * part * 256 * 256),
            bytes_accessed=2 * 1024 * 1024,
            transcendentals=0,
        ),
        name="denoise_" + stage,
    )(*operands)


def rotation(count, step):
    return [(i, (i + step) % count) for i in range(count)]


def swaps(count, first):
    pairs = [(i, (i + 1) % count) for i in range(first, count, 2)]
    return pairs + [(target, source) for source, target in pairs]


def exchanged(values, axis, count):
    arrived = {0: values[0]}
    for k in sorted(range(1, count), key=lambda k: abs(k - count / 2)):
        arrived[k] = lax.ppermute(values[k], axis, rotation(count, k))
    return [arrived[k] for k in range(count)]


def per_device(initial, coil_maps, kspace, sampled, first_w, time_w, last_w):
    section_no = lax.axis_index("cascade")
    sections = lax.axis_size("cascade")
    shares = lax.axis_size("coil")
    readout_parts = lax.axis_size("readout")
    phases = kspace.shape[2]
    part = kspace.shape[-1]
    channels = first_w.shape[-1]

    def rows_of(array):
        return array.reshape(array.shape[:-3] + (2 * array.shape[-3], part))

    def padded(block):
        return jnp.pad(block, ((0, -block.shape[0] % 64), (0, 0)))

    initial, coil_maps, kspace = rows_of(initial), rows_of(coil_maps), rows_of(kspace)
    images = {"all": [initial]}
    matrices = None
    joints = []

    def in_order(near, far, axis):
        return jnp.where(
            far_is_up(),
            jnp.concatenate([near, far], axis),
            jnp.concatenate([far, near], axis),
        )

    for section in range(sections):
        parts = {}
        for side, image in images.items():
            partial = consistency(image, coil_maps, kspace, sampled, shares, side)
            if matrices is None:
                partial, (first_w, time_w, last_w) = lax.optimization_barrier(
                    (partial, (first_w, time_w, last_w))
                )
            parts[side] = exchanged(partial, "coil", shares)
        if matrices is None:
            pack = jnp.concatenate(
                [
                    time_w[0].reshape(-1, channels),
                    padded(first_w[0].reshape(-1, channels)),
                    padded(jnp.swapaxes(last_w[0], 1, 2).reshape(-1, channels)),
                ],
                0,
            )
            packs = exchanged([pack] * sections, "cascade", sections)
            matrices = weight_matrices(packs, phases)
            parts, matrices = lax.optimization_barrier((parts, matrices))
        added = {
            side: sum(p.astype(F32) for p in pieces).astype(BF16) for side, pieces in parts.items()
        }
        combined = added["all"] if section == 0 else in_order(added["near"], added["far"], 0)
        even = lax.ppermute(combined, "readout", swaps(readout_parts, 0))
        odd = lax.ppermute(combined, "readout", swaps(readout_parts, 1))
        (sums,) = denoise("alone", combined, matrices, section, phases)
        (sums,) = denoise("near", combined, matrices, section, phases, even, sums)
        if section < sections - 1:
            near, rest = denoise("far", combined, matrices, section, phases, odd, sums)
            far, joint = denoise("last", combined, matrices, section, phases, odd, rest, near)
            images = {
                side: exchanged([value] * shares, "coil", shares)
                for side, value in (("near", near), ("far", far))
            }

        else:
            (joint,) = denoise("end", combined, matrices, section, phases, odd, sums)
        joints.append(joint)

    def of_section(values, wanted):
        value = values[0]
        for section in range(1, sections):
            value = jnp.where(wanted == section, values[section], value)
        return value

    pieces = exchanged(
        [of_section(joints, (section_no + k) % sections) for k in range(sections)],
        "cascade",
        sections,
    )
    result = jnp.zeros((sections,) + joints[0].shape, BF16)
    for k in range(sections):
        place = lax.rem(section_no - k + sections, sections)
        result = lax.dynamic_update_slice_in_dim(result, pieces[k][None], place, 0)
    result = result[None]
    return result.reshape(result.shape[:-2] + (result.shape[-2] // 2, 2, part))


def solution(mesh):
    in_specs = (
        P(None, None, "readout", None, None, None),
        P(None, "coil", "readout", None, None, None),
        P(None, "coil", None, "readout", None, None, None),
        P("coil", None, None, None),
        P("cascade", None, None, None),
        P("cascade", None, None, None),
        P("cascade", None, None, None),
    )
    out_specs = P("cascade", None, None, "readout", "coil", None, None)
    return jax.shard_map(
        per_device, mesh=mesh, in_specs=in_specs, out_specs=out_specs, check_vma=False
    )
```
